256 devices in a mesh: cam: 4 (over y_hi, core), frame: 64 (over y_lo, z, x).
Axes of the slice: x: 4, y: 4 (y_hi: 2, y_lo: 2; y = y_hi * 2 + y_lo), z: 8, core: 2. Of those that a mesh axis runs over, the one named last changes fastest.
Arguments:
- tokens: bfloat16 [8, 64, 256, 1152], P('cam', 'frame'), may hold values from -6 to 6
- counts: int32 [8, 64], P('cam', 'frame'), may hold values from 1 to 4, as said below
- neighbours: int32 [8, 2], P('cam'), may hold values from 0 to 7, as said below
- side_keys: bfloat16 [2, 576], replicated, may hold values from -5 to 5
- cross_qkv: bfloat16 [1152, 1728], replicated, may hold values from -2 to 2
- cross_out: bfloat16 [576, 1152], replicated, may hold values from -0.25 to 0.25
- time_qkv: bfloat16 [1152, 1728], replicated, may hold values from -2 to 2
- time_out: bfloat16 [576, 1152], replicated, may hold values from -0.25 to 0.25
Outputs:
- block_output: bfloat16 [8, 64, 256, 1152], P('cam', 'frame')
The draws below stay inside these ranges and needn't reach their ends.
Inputs may be any that keep to these rules, and one draw needn't show every extreme that they name: `counts`: in every camera some frame is full, with 4 rows. Row c holds camera c's cycle neighbours (c - 1) mod 8 and (c + 1) mod 8, in either order.
All inputs are finite; a program needn't handle non-finite values.
Results may differ from the reference program's by a relative error of at most 0.017.
The reference program's roundings to bfloat16 on the way count: a program that leaves them out, or rounds other values in their place, can miss the bound.
Values may be sent and summed in bfloat16 or wider, within the bound.
No kernel may reach another device: no remote copies, remote signals or barrier semaphores. Data moves between devices by JAX's collectives and lax.ppermute only.
A program may use at most 128 MiB of HBM per device.

```python
import jax
import jax.numpy as jnp
from jax import lax

D = 1152
HEADS = 8
HEAD_DIM = 72
INNER = 576
TOK = 256
CAMS = 8
FRAMES = 64


def weight_matrix(key, strength):
    spread = (D // 4) ** (-0.5)
    shape = (D, 3 * INNER)
    key = jax.random.fold_in(key, strength)
    result = jnp.clip(jax.random.normal(key, shape, jnp.float32), -6.0, 6.0) * spread
    return result


def draw_cross_qkv(key, part):
    return weight_matrix(key, 300).astype(jnp.bfloat16)


def draw_time_qkv(key, part):
    return weight_matrix(key, 600).astype(jnp.bfloat16)


def draw_tokens(key, part):
    shape = (CAMS, FRAMES, TOK, D)
    key = jax.random.fold_in(key, 5)
    result = jnp.clip(jax.random.normal(key, shape, jnp.float32), -6.0, 6.0)
    return result.astype(jnp.bfloat16)


def draw_counts(key, part):
    key = jax.random.fold_in(key, 11)
    first_key, second_key = jax.random.split(key)
    most_rows = TOK // 64
    base = jax.random.randint(first_key, (CAMS, FRAMES), 1, most_rows + 1)
    full_frame = jax.random.randint(second_key, (CAMS, 1), 0, FRAMES)
    frame_ids = jnp.arange(FRAMES, dtype=jnp.int32)[None, :]
    return jnp.where(frame_ids == full_frame, most_rows, base).astype(jnp.int32)


def draw_neighbours(key, part):
    key = jax.random.fold_in(key, 23)
    flips = jax.random.randint(key, (CAMS,), 0, 2)
    cam_ids = jnp.arange(CAMS, dtype=jnp.int32)
    lower = (cam_ids - 1) % CAMS
    upper = (cam_ids + 1) % CAMS
    first = jnp.where(flips == 1, upper, lower)
    second = jnp.where(flips == 1, lower, upper)
    return jnp.stack([first, second], axis=1).astype(jnp.int32)


def scatter_about(own_key, dims, scale, most, kind=jnp.bfloat16):
    return jnp.clip(scale * jax.random.normal(own_key, dims, jnp.float32), -most, most).astype(kind)


def setup_inputs(seed: int = 0) -> dict:
    splits = jax.random.split(jax.random.key(seed), 9)
    tokens = draw_tokens(jax.random.fold_in(splits[8], 71), 0)
    counts = draw_counts(jax.random.fold_in(splits[8], 71), 0)
    neighbours = draw_neighbours(jax.random.fold_in(splits[8], 71), 0)
    side_keys = scatter_about(splits[3], (2, INNER), 1.0, 5.0)
    cross_qkv = draw_cross_qkv(jax.random.fold_in(splits[8], 71), 0)
    cross_out = scatter_about(splits[5], (INNER, D), INNER ** -0.5, 0.25)
    time_qkv = draw_time_qkv(jax.random.fold_in(splits[8], 71), 0)
    time_out = scatter_about(splits[7], (INNER, D), INNER ** -0.5, 0.25)
    return dict(tokens=tokens, counts=counts, neighbours=neighbours, side_keys=side_keys, cross_qkv=cross_qkv, cross_out=cross_out, time_qkv=time_qkv, time_out=time_out)


epsilon = 1e-06
row_tokens = 64

def normalize(values):
    values = values.astype(jnp.float32)
    mean = lax.optimization_barrier(jnp.mean(values, axis=-1, keepdims=True))
    centred = values - mean
    variance = lax.optimization_barrier(jnp.mean(centred * centred, axis=-1, keepdims=True))
    return (centred * lax.rsqrt(variance + epsilon)).astype(jnp.bfloat16)

def project(normed, weight):
    flat = normed.reshape(-1, normed.shape[-1])
    result = jnp.dot(flat, weight, preferred_element_type=jnp.float32)
    return result.reshape(normed.shape[:-1] + (weight.shape[1],))

def softmax_rows(scores, allowed):
    masked = jnp.where(allowed, scores, -1e+30)
    highest = lax.optimization_barrier(jnp.max(masked, axis=-1, keepdims=True))
    expo = jnp.exp(masked - highest)
    return (expo / lax.optimization_barrier(jnp.sum(expo, axis=-1, keepdims=True))).astype(jnp.bfloat16)

def reference(tokens, counts, neighbours, side_keys, cross_qkv, cross_out, time_qkv, time_out):
    cameras, frames, token_count, width = tokens.shape
    inner = HEADS * HEAD_DIM
    scale = HEAD_DIM ** (-0.5)
    position = jnp.arange(token_count, dtype=jnp.int32)
    valid = position[None, None, :] < row_tokens * counts[:, :, None]

    def cross_project(camera_tokens):
        return project(normalize(camera_tokens), cross_qkv).astype(jnp.bfloat16)
    projected = lax.map(cross_project, tokens)
    query = projected[..., :inner]
    keys = projected[..., inner:2 * inner]
    values = projected[..., 2 * inner:]
    cam_ids = jnp.arange(cameras, dtype=jnp.int32)
    lower = (cam_ids - 1) % cameras
    upper = (cam_ids + 1) % cameras
    first_lower = neighbours[:, 0] == lower
    side_lower = jnp.where(first_lower[:, None], side_keys[0][None], side_keys[1][None]).astype(jnp.float32)
    side_upper = jnp.where(first_lower[:, None], side_keys[1][None], side_keys[0][None]).astype(jnp.float32)
    lower_keys = (keys[lower].astype(jnp.float32) + side_lower[:, None, None, :]).astype(jnp.bfloat16)
    upper_keys = (keys[upper].astype(jnp.float32) + side_upper[:, None, None, :]).astype(jnp.bfloat16)
    all_keys = jnp.concatenate([keys, lower_keys, upper_keys], axis=2)
    all_values = jnp.concatenate([values, values[lower], values[upper]], axis=2)
    all_valid = jnp.concatenate([valid, valid[lower], valid[upper]], axis=2)

    def cross_one(pieces):
        one_query, one_keys, one_values, one_valid = pieces
        query_heads = one_query.reshape(token_count, HEADS, HEAD_DIM).astype(jnp.float32)
        key_heads = one_keys.reshape(3 * token_count, HEADS, HEAD_DIM).astype(jnp.float32)
        value_heads = one_values.reshape(3 * token_count, HEADS, HEAD_DIM).astype(jnp.float32)
        scores = jnp.einsum('qhd,khd->hqk', query_heads, key_heads) * scale
        probs = softmax_rows(scores, one_valid[None, None, :])
        attended = jnp.einsum('hqk,khd->qhd', probs.astype(jnp.float32), value_heads)
        return attended.reshape(token_count, inner).astype(jnp.bfloat16)
    flat_count = cameras * frames
    attended = lax.map(cross_one, (query.reshape(flat_count, token_count, inner), all_keys.reshape(flat_count, 3 * token_count, inner), all_values.reshape(flat_count, 3 * token_count, inner), all_valid.reshape(flat_count, 3 * token_count)))
    attended = attended.reshape(cameras, frames, token_count, inner)
    mixed = (project(attended, cross_out) + tokens.astype(jnp.float32)).astype(jnp.bfloat16)

    def time_project(camera_tokens):
        return project(normalize(camera_tokens), time_qkv).astype(jnp.bfloat16)
    time_proj = lax.map(time_project, mixed)
    same_frame = jnp.eye(frames, dtype=jnp.bool_)

    def time_one(pieces):
        one_proj, one_valid = pieces
        query_heads = one_proj[..., :inner].reshape(frames, token_count, HEADS, HEAD_DIM).astype(jnp.float32)
        key_heads = one_proj[..., inner:2 * inner].reshape(frames, token_count, HEADS, HEAD_DIM).astype(jnp.float32)
        value_heads = one_proj[..., 2 * inner:].reshape(frames, token_count, HEADS, HEAD_DIM).astype(jnp.float32)
        scores = jnp.einsum('fthd,gthd->thfg', query_heads, key_heads) * scale
        allowed = jnp.transpose(one_valid)[:, None, None, :] | same_frame[None, None]
        probs = softmax_rows(scores, allowed)
        attended_time = jnp.einsum('thfg,gthd->fthd', probs.astype(jnp.float32), value_heads)
        return attended_time.reshape(frames, token_count, inner).astype(jnp.bfloat16)
    time_attended = lax.map(time_one, (time_proj, valid))
    result = project(time_attended, time_out) + mixed.astype(jnp.float32)
    return result.astype(jnp.bfloat16)
```

```python
import functools
import math

import jax
import jax.numpy as jnp
from jax import lax
from jax.experimental import pallas as pl
from jax.experimental.pallas import tpu as pltpu
from jax.sharding import PartitionSpec as P

HEADS = 8
HEAD = 72
INNER = HEADS * HEAD
EPS = 1e-06
ROW_TOKENS = 64
BIG = 1e30
COEF = HEAD ** (-0.5) * math.log2(math.e)
LANES = 128
MIB = 1 << 20


def passed_along(x, axis, by):
    peers = lax.axis_size(axis)
    return lax.ppermute(x, axis, [(i, (i + by) % peers) for i in range(peers)])


def dot_nt(a, b):
    return lax.dot_general(a, b, (((1,), (1,)), ((), ())), preferred_element_type=jnp.float32)


def dot_nn(a, b):
    return lax.dot_general(a, b, (((1,), (0,)), ((), ())), preferred_element_type=jnp.float32)


def normalize(values):
    values = values.astype(jnp.float32)
    mean = jnp.mean(values, axis=-1, keepdims=True)
    centred = values - mean
    variance = jnp.mean(centred * centred, axis=-1, keepdims=True)
    return (centred * lax.rsqrt(variance + EPS)).astype(jnp.bfloat16)


def lane_ids(rows):
    return lax.broadcasted_iota(jnp.int32, (rows, LANES), 1)


def row_ids(rows):
    return lax.broadcasted_iota(jnp.int32, (rows, LANES), 0)


def invalid_bias(rows, count):
    return jnp.where(row_ids(rows) < ROW_TOKENS * count, 0.0, -BIG).astype(jnp.bfloat16)


def query_window(x, head):
    window = x[:, head * HEAD : head * HEAD + LANES]
    return jnp.where(lane_ids(x.shape[0]) == HEAD, jnp.ones_like(window), window)


def key_window(x, start, bias):
    window = x[:, start : start + LANES]
    lane = lane_ids(x.shape[0])
    return jnp.where(lane < HEAD, window, jnp.where(lane == HEAD, bias, jnp.zeros_like(window)))


def value_window(x, start):
    window = x[:, start : start + LANES]
    return jnp.where(lane_ids(x.shape[0]) == HEAD, jnp.ones_like(window), window)


def join_heads(pieces):
    return jnp.concatenate([piece[:, :HEAD] for piece in pieces], axis=1)


def side_row(side_ref, neighbours_ref, cam, lower, cameras, cam_here):
    camera = lax.axis_index("cam") * cam_here + cam
    first_lower = neighbours_ref[cam, 0] == lax.rem(camera + cameras - 1, cameras)
    pick_first = first_lower if lower else jnp.logical_not(first_lower)
    return jnp.where(pick_first, side_ref[0:1, :], side_ref[1:2, :])


def local_kernel(cameras, counts_ref, neighbours_ref, tokens_ref, weight_ref, side_ref, query_ref, part_ref, qkv_ref):
    rows = tokens_ref.shape[0] // 2
    normed = normalize(tokens_ref[...])
    width = weight_ref.shape[0]
    qkv_ref[:, :width] = dot_nt(normed, weight_ref[...]).astype(jnp.bfloat16)
    qkv_ref[:, width:] = jnp.zeros((2 * rows, qkv_ref.shape[1] - width), jnp.bfloat16)
    query_ref[...] = qkv_ref[:, : query_ref.shape[1]]
    biases = [invalid_bias(rows, counts_ref[c, 0]) for c in range(2)]
    for c in range(2):
        own, other = pl.ds(c * rows, rows), pl.ds((1 - c) * rows, rows)
        side = side_row(side_ref, neighbours_ref, c, c == 1, cameras, 2)
        q_all = qkv_ref[own, :640]
        k_own = qkv_ref[own, 512:1280]
        k_other = qkv_ref[other, 512:1280]
        k_other = (k_other.astype(jnp.float32) + side).astype(jnp.bfloat16)
        v_own, v_other = qkv_ref[own, 1152:], qkv_ref[other, 1152:]
        for h in range(HEADS):
            q = query_window(q_all, h)
            start = INNER - 512 + h * HEAD
            k = jnp.concatenate(
                [key_window(k_own, start, biases[c]), key_window(k_other, start, biases[1 - c])], axis=0
            )
            v = jnp.concatenate([value_window(v_own, h * HEAD), value_window(v_other, h * HEAD)], axis=0)
            scores = dot_nt(q, k)
            highest = jnp.max(scores, axis=1, keepdims=True)
            expo = jnp.exp2((scores - highest) * COEF).astype(jnp.bfloat16)
            summed = dot_nn(expo, v)
            part_ref[c, h] = jnp.where(lane_ids(rows) == HEAD + 1, highest, summed)


def merge_kernel(
    cameras, counts_ref, far_counts_ref, neighbours_ref, tokens_ref, lower_ref, upper_ref, weight_ref, side_ref, query_ref,
    part_ref, out_weight_ref, mixed_ref, payload_ref, kv_ref,
):
    rows = tokens_ref.shape[0] // 2
    kv_weight = weight_ref[INNER:, :]
    for c, far_ref in enumerate((lower_ref, upper_ref)):
        here = pl.ds(c * rows, rows)
        kv_ref[here, : 2 * INNER] = dot_nt(normalize(far_ref[...]), kv_weight).astype(jnp.bfloat16)
        kv_ref[here, 2 * INNER :] = jnp.zeros((rows, kv_ref.shape[1] - 2 * INNER), jnp.bfloat16)
    for c in range(2):
        here = pl.ds(c * rows, rows)
        side = side_row(side_ref, neighbours_ref, c, c == 0, cameras, 2)
        bias = invalid_bias(rows, far_counts_ref[c, 0])
        q_all = query_ref[here, :]
        k_all = (kv_ref[here, : 640].astype(jnp.float32) + side).astype(jnp.bfloat16)
        v_all = kv_ref[here, 512:]
        pieces = []
        for h in range(HEADS):
            q = query_window(q_all, h)
            k = key_window(k_all, h * HEAD, bias)
            v = value_window(v_all, INNER - 512 + h * HEAD)
            scores = dot_nt(q, k)
            part = part_ref[c, h]
            before = part[:, HEAD + 1 : HEAD + 2]
            highest = jnp.maximum(jnp.max(scores, axis=1, keepdims=True), before)
            expo = jnp.exp2((scores - highest) * COEF).astype(jnp.bfloat16)
            summed = part * jnp.exp2((before - highest) * COEF) + dot_nn(expo, v)
            pieces.append(summed / summed[:, HEAD : HEAD + 1])
        attended = join_heads(pieces).astype(jnp.bfloat16)
        mixed = dot_nn(attended, out_weight_ref[...]) + tokens_ref[here, :].astype(jnp.float32)
        mixed = mixed.astype(jnp.bfloat16)
        mixed_ref[here, :] = mixed
        width = mixed.shape[1]
        payload_ref[here, :width] = normalize(mixed)
        valid = row_ids(rows) < ROW_TOKENS * counts_ref[c, 0]
        payload_ref[here, width:] = jnp.where(valid, 1.0, 0.0).astype(jnp.bfloat16)


def time_kernel(frames, payload_ref, weight_ref, out_ref, qkv_ref):
    rows = payload_ref.shape[0]
    places = rows // frames
    width = weight_ref.shape[0]
    model = weight_ref.shape[1]
    qkv_ref[:, :width] = dot_nt(payload_ref[:, :model], weight_ref[...]).astype(jnp.bfloat16)
    qkv_ref[:, width:] = jnp.zeros((rows, qkv_ref.shape[1] - width), jnp.bfloat16)
    lane = lane_ids(rows)
    frame = row_ids(rows) // places
    place = row_ids(rows) % places
    invalid = payload_ref[:, model:].astype(jnp.float32) < 0.5
    query_mask = jnp.where(
        lane < frames,
        jnp.where(lane == frame, 1.0, 0.0),
        jnp.where(jnp.logical_and(lane < frames + places, lane - frames != place), -BIG, 0.0),
    ).astype(jnp.bfloat16)
    key_mask = jnp.where(
        lane < frames,
        jnp.where(jnp.logical_and(invalid, lane != frame), -BIG, 0.0),
        jnp.where(lane - frames == place, 1.0, 0.0),
    ).astype(jnp.bfloat16)
    zero = jnp.zeros((rows, LANES), jnp.bfloat16)
    q_all, k_all, v_all = qkv_ref[:, :640], qkv_ref[:, 512:1280], qkv_ref[:, 1152:]
    block = 256
    ks, vs = [], []
    pieces = [[] for _ in range(rows // block)]
    for h in range(HEADS):
        k = jnp.concatenate([key_window(k_all, INNER - 512 + h * HEAD, zero), key_mask], axis=1)
        v = value_window(v_all, h * HEAD)
        q = jnp.concatenate([q_all[:, h * HEAD : h * HEAD + LANES], query_mask], axis=1)
        for b in range(rows // block):
            scores = dot_nt(q[b * block : (b + 1) * block], k)
            highest = jnp.max(scores, axis=1, keepdims=True)
            expo = jnp.exp2((scores - highest) * COEF).astype(jnp.bfloat16)
            summed = dot_nn(expo, v)
            pieces[b].append(summed / summed[:, HEAD : HEAD + 1])
    for b in range(rows // block):
        out_ref[b * block : (b + 1) * block, :] = join_heads(pieces[b]).astype(jnp.bfloat16)


def final_kernel(attended_ref, weight_ref, mixed_ref, out_ref):
    result = dot_nn(attended_ref[...], weight_ref[...]) + mixed_ref[...].astype(jnp.float32)
    out_ref[...] = result.astype(jnp.bfloat16)


SMEM = pl.BlockSpec(memory_space=pltpu.SMEM)
VMEM = pl.BlockSpec(memory_space=pltpu.VMEM)


def kernel_call(body, ins, outs, scratch, mib, flops, nbytes):
    return pl.pallas_call(
        body,
        out_shape=outs,
        in_specs=ins,
        out_specs=[VMEM] * len(outs),
        scratch_shapes=scratch,
        compiler_params=pltpu.CompilerParams(vmem_limit_bytes=mib * MIB),
        cost_estimate=pl.CostEstimate(flops=flops, bytes_accessed=nbytes, transcendentals=0),
    )


def shards(tokens, counts, neighbours, side_keys, cross_qkv, cross_out, time_qkv, time_out):
    cam_here, frames_here, token_count, model = tokens.shape
    cameras = cam_here * lax.axis_size("cam")
    frames = lax.axis_size("frame")
    rows = cam_here * token_count
    bf16 = jnp.bfloat16
    spread = functools.partial(jax.ShapeDtypeStruct, dtype=bf16)

    lower_count = passed_along(counts[-1:], "cam", 1)
    upper_count = passed_along(counts[:1], "cam", -1)
    lower = passed_along(tokens[-1, 0], "cam", 1)
    upper = passed_along(tokens[0, 0], "cam", -1)
    far_counts = jnp.concatenate([lower_count, upper_count], axis=0)

    flat = tokens.reshape(rows, model)
    cross_t, time_t = cross_qkv.T, time_qkv.T
    side_local = jnp.pad(side_keys.astype(jnp.float32), ((0, 0), (INNER - 512, 128)))
    side_far = jnp.pad(side_keys.astype(jnp.float32), ((0, 0), (0, 64)))

    query, part = kernel_call(
        functools.partial(local_kernel, cameras),
        [SMEM, SMEM, VMEM, VMEM, VMEM],
        [spread((rows, 640)), jax.ShapeDtypeStruct((2, HEADS, token_count, LANES), jnp.float32)],
        [pltpu.VMEM((rows, 1792), bf16)],
        32,
        6_000_000_000,
        20_000_000,
    )(counts, neighbours, flat, cross_t, side_local)

    mixed, payload = kernel_call(
        functools.partial(merge_kernel, cameras),
        [SMEM, SMEM, SMEM] + [VMEM] * 8,
        [spread((rows, model)), spread((rows, model + LANES))],
        [pltpu.VMEM((rows, 1280), bf16)],
        32,
        4_000_000_000,
        12_000_000,
    )(counts, far_counts, neighbours, flat, lower, upper, cross_t, side_far, query, part, cross_out)

    chunk = rows // frames
    arrived = lax.all_to_all(
        payload.reshape(frames, chunk, model + LANES), "frame", split_axis=0, concat_axis=0, tiled=True
    )
    (attended,) = kernel_call(
        functools.partial(time_kernel, frames),
        [VMEM] * 2,
        [spread((rows, INNER))],
        [pltpu.VMEM((rows, 1792), bf16)],
        32,
        6_000_000_000,
        10_000_000,
    )(arrived.reshape(rows, model + LANES), time_t)
    returned = lax.all_to_all(
        attended.reshape(frames, chunk, INNER), "frame", split_axis=0, concat_axis=0, tiled=True
    )
    (out,) = kernel_call(
        final_kernel,
        [VMEM] * 3,
        [spread((rows, model))],
        [],
        32,
        700_000_000,
        4_000_000,
    )(returned.reshape(rows, INNER), time_out, mixed)
    return out.reshape(tokens.shape)


def solution(mesh):
    return jax.shard_map(
        shards,
        mesh=mesh,
        in_specs=(
            P("cam", "frame", None, None),
            P("cam", "frame"),
            P("cam", None),
            P(),
            P(),
            P(),
            P(),
            P(),
        ),
        out_specs=P("cam", "frame", None, None),
        check_vma=False,
    )
```

```python
import functools
import math

import jax
import jax.numpy as jnp
from jax import lax
from jax.experimental import pallas as pl
from jax.experimental.pallas import tpu as pltpu
from jax.sharding import PartitionSpec as P

HEADS = 8
HEAD = 72
INNER = HEADS * HEAD
EPS = 1e-06
ROW_TOKENS = 64
BIG = 1e30
COEF = HEAD ** (-0.5) * math.log2(math.e)
LANES = 128
KEY_LANES = 640
MIB = 1 << 20


def passed_along(x, axis, by):
    peers = lax.axis_size(axis)
    return lax.ppermute(x, axis, [(i, (i + by) % peers) for i in range(peers)])


def dot_nt(a, b):
    return lax.dot_general(a, b, (((1,), (1,)), ((), ())), preferred_element_type=jnp.float32)


def dot_nn(a, b):
    return lax.dot_general(a, b, (((1,), (0,)), ((), ())), preferred_element_type=jnp.float32)


def normalize(values):
    values = values.astype(jnp.float32)
    mean = jnp.mean(values, axis=-1, keepdims=True)
    centred = values - mean
    variance = jnp.mean(centred * centred, axis=-1, keepdims=True)
    return (centred * lax.rsqrt(variance + EPS)).astype(jnp.bfloat16)


def keys_bias(rows, count):
    position = lax.broadcasted_iota(jnp.int32, (rows, LANES), 0)
    return jnp.where(position < ROW_TOKENS * count, 0.0, -BIG).astype(jnp.bfloat16)


def key_window(keys, head, bias):
    window = keys[:, head * HEAD : head * HEAD + LANES]
    lane = lax.broadcasted_iota(jnp.int32, window.shape, 1)
    window = jnp.where(lane < HEAD, window, jnp.zeros_like(window))
    return window if bias is None else jnp.where(lane == HEAD, bias, window)


def one_then_zeros(rows, columns):
    return jnp.where(lax.broadcasted_iota(jnp.int32, (rows, columns), 0) == 0, 1.0, 0.0)


def head_rows(x, head):
    return x[head * HEAD : (head + 1) * HEAD, :]


def rounded(x):
    return x.astype(jnp.bfloat16).astype(jnp.float32)


def padded_keys(keys):
    fill = jnp.zeros((keys.shape[0], KEY_LANES - keys.shape[1]), jnp.float32)
    return jnp.concatenate([keys, fill], axis=1).astype(jnp.bfloat16)


def with_side(keys, side):
    return (keys.astype(jnp.float32) + side).astype(jnp.bfloat16)


def side_row(side_ref, neighbours_ref, cam, lower, cameras, cam_here):
    camera = lax.axis_index("cam") * cam_here + cam
    first_lower = neighbours_ref[cam, 0] == lax.rem(camera + cameras - 1, cameras)
    pick_first = first_lower if lower else jnp.logical_not(first_lower)
    return jnp.where(pick_first, side_ref[0:1, :], side_ref[1:2, :])


def staggered(items, score, rest, ahead):
    scores = [score(item) for item in items[:ahead]]
    for i, item in enumerate(items):
        if i + ahead < len(items):
            scores.append(score(items[i + ahead]))
        rest(item, scores[i])
        scores[i] = None


def norm_kernel(tokens_ref, first_ref, second_ref):
    rows = first_ref.shape[0]
    first_ref[...] = normalize(tokens_ref[:rows, :])
    second_ref[...] = normalize(tokens_ref[rows:, :])


def local_kernel(
    cameras, counts_ref, neighbours_ref, first_ref, second_ref, weight_ref, side_ref, query_ref, part_ref, value_ref
):
    rows = first_ref.shape[0]
    normed = jnp.concatenate([first_ref[...], second_ref[...]], axis=0)
    keys = padded_keys(dot_nt(normed, weight_ref[INNER : 2 * INNER, :]))
    query_ref[...] = rounded(dot_nt(weight_ref[:INNER, :], normed))
    value_ref[...] = rounded(dot_nt(weight_ref[2 * INNER :, :], normed))
    biases = [keys_bias(rows, counts_ref[c, 0]) for c in range(2)]
    one_rows = one_then_zeros(LANES - HEAD, rows)
    value_ones = one_then_zeros(8, 2 * rows)
    kept = []
    for c in range(2):
        own, other = slice(c * rows, (c + 1) * rows), slice((1 - c) * rows, (2 - c) * rows)
        side = side_row(side_ref, neighbours_ref, c, c == 1, cameras, 2)
        kept.append(
            (
                own,
                other,
                jnp.concatenate([keys[own], with_side(keys[other], side)], axis=0),
                jnp.concatenate([biases[c], biases[1 - c]], axis=0),
            )
        )

    def score(item):
        c, h = item
        own, _, k_all, bias = kept[c]
        q = jnp.concatenate([head_rows(query_ref[:, own], h), one_rows], axis=0).astype(jnp.bfloat16)
        return dot_nn(key_window(k_all, h, bias), q)

    def rest(item, scores):
        c, h = item
        own, other, _, _ = kept[c]
        highest = jnp.max(scores, axis=0, keepdims=True)
        expo = jnp.exp2((scores - highest) * COEF).astype(jnp.bfloat16)
        v = jnp.concatenate([head_rows(value_ref[:, own], h), head_rows(value_ref[:, other], h)], axis=1)
        summed = dot_nn(jnp.concatenate([v, value_ones], axis=0).astype(jnp.bfloat16), expo)
        row = lax.broadcasted_iota(jnp.int32, summed.shape, 0)
        part_ref[c, h] = jnp.where(row == HEAD + 1, highest, summed)

    staggered([(c, h) for c in range(2) for h in range(HEADS)], score, rest, 3)


def merge_kernel(
    cameras, counts_ref, lower_counts_ref, upper_counts_ref, neighbours_ref, tokens_ref, lower_ref, upper_ref, weight_ref,
    side_ref, query_ref, part_ref, out_weight_ref, mixed_ref, payload_ref, value_ref,
):
    rows = lower_ref.shape[0]
    far = jnp.concatenate([lower_ref[...], upper_ref[...]], axis=0)
    keys = padded_keys(dot_nt(far, weight_ref[INNER : 2 * INNER, :]))
    value_ref[...] = rounded(dot_nt(weight_ref[2 * INNER :, :], far))
    one_rows = one_then_zeros(LANES - HEAD, rows)
    value_ones = one_then_zeros(8, rows)
    far_counts = (lower_counts_ref[1, 0], upper_counts_ref[0, 0])
    kept = []
    for c in range(2):
        here = slice(c * rows, (c + 1) * rows)
        side = side_row(side_ref, neighbours_ref, c, c == 0, cameras, 2)
        kept.append((here, with_side(keys[here], side), keys_bias(rows, far_counts[c])))
    pieces = [[], []]

    def score(item):
        c, h = item
        here, k_all, bias = kept[c]
        q = jnp.concatenate([head_rows(query_ref[:, here], h), one_rows], axis=0).astype(jnp.bfloat16)
        return dot_nn(key_window(k_all, h, bias), q)

    def rest(item, scores):
        c, h = item
        here = kept[c][0]
        part = part_ref[c, h]
        before = part[HEAD + 1 : HEAD + 2, :]
        highest = jnp.maximum(jnp.max(scores, axis=0, keepdims=True), before)
        expo = jnp.exp2((scores - highest) * COEF).astype(jnp.bfloat16)
        v = jnp.concatenate([head_rows(value_ref[:, here], h), value_ones], axis=0).astype(jnp.bfloat16)
        summed = part * jnp.exp2((before - highest) * COEF) + dot_nn(v, expo)
        pieces[c].append(summed[:HEAD] * (1.0 / summed[HEAD : HEAD + 1]))

    staggered([(c, h) for c in range(2) for h in range(HEADS)], score, rest, 3)
    for c in range(2):
        here = slice(c * rows, (c + 1) * rows)
        attended = jnp.concatenate(pieces[c], axis=0).T.astype(jnp.bfloat16)
        mixed = dot_nn(attended, out_weight_ref[...]) + tokens_ref[here, :].astype(jnp.float32)
        mixed = mixed.astype(jnp.bfloat16)
        mixed_ref[here, :] = mixed
        width = mixed.shape[1]
        payload_ref[here, :width] = normalize(mixed)
        position = lax.broadcasted_iota(jnp.int32, (rows, LANES), 0)
        valid = position < ROW_TOKENS * counts_ref[c, 0]
        payload_ref[here, width:] = jnp.where(valid, 1.0, 0.0).astype(jnp.bfloat16)


def time_kernel(frames, payload_ref, weight_ref, out_ref, query_ref, value_ref):
    rows = payload_ref.shape[0]
    places = rows // frames
    model = weight_ref.shape[1]
    normed = payload_ref[:, :model]
    keys = padded_keys(dot_nt(normed, weight_ref[INNER : 2 * INNER, :]))
    query_ref[...] = rounded(dot_nt(weight_ref[:INNER, :], normed))
    value_ref[...] = rounded(dot_nt(weight_ref[2 * INNER :, :], normed))
    lane = lax.broadcasted_iota(jnp.int32, (rows, LANES), 1)
    key = lax.broadcasted_iota(jnp.int32, (rows, LANES), 0)
    invalid = payload_ref[:, model:].astype(jnp.float32) < 0.5
    key_mask = jnp.where(
        lane < frames,
        jnp.where(jnp.logical_and(invalid, lane != key // places), -BIG, 0.0),
        jnp.where(lane - frames == key % places, 1.0, 0.0),
    ).astype(jnp.bfloat16)
    entry = lax.broadcasted_iota(jnp.int32, (LANES, rows), 0)
    query = lax.broadcasted_iota(jnp.int32, (LANES, rows), 1)
    query_mask = jnp.where(
        entry < frames,
        jnp.where(entry == query // places, 1.0, 0.0),
        jnp.where(jnp.logical_and(entry < frames + places, entry - frames != query % places), -BIG, 0.0),
    ).astype(jnp.bfloat16)
    zero_rows = jnp.zeros((LANES - HEAD, rows), jnp.float32)
    value_ones = one_then_zeros(8, rows)
    block = 256
    blocks = rows // block
    pieces = [[] for _ in range(blocks)]

    def score(item):
        h, b = item
        here = slice(b * block, (b + 1) * block)
        q = jnp.concatenate([head_rows(query_ref[:, here], h), zero_rows[:, here]], axis=0).astype(jnp.bfloat16)
        return dot_nn(
            jnp.concatenate([key_window(keys, h, None), key_mask], axis=1),
            jnp.concatenate([q, query_mask[:, here]], axis=0),
        )

    def rest(item, scores):
        h, b = item
        highest = jnp.max(scores, axis=0, keepdims=True)
        expo = jnp.exp2((scores - highest) * COEF).astype(jnp.bfloat16)
        v = jnp.concatenate([head_rows(value_ref[...], h), value_ones], axis=0).astype(jnp.bfloat16)
        summed = dot_nn(v, expo)
        pieces[b].append(summed[:HEAD] * (1.0 / summed[HEAD : HEAD + 1]))

    staggered([(h, b) for h in range(HEADS) for b in range(blocks)], score, rest, 3)
    for b in range(blocks):
        out_ref[b * block : (b + 1) * block, :] = jnp.concatenate(pieces[b], axis=0).T.astype(jnp.bfloat16)


def final_kernel(attended_ref, weight_ref, mixed_ref, out_ref):
    result = dot_nn(attended_ref[...], weight_ref[...]) + mixed_ref[...].astype(jnp.float32)
    out_ref[...] = result.astype(jnp.bfloat16)


SMEM = pl.BlockSpec(memory_space=pltpu.SMEM)
VMEM = pl.BlockSpec(memory_space=pltpu.VMEM)


def kernel_call(body, ins, outs, scratch, mib, flops, nbytes):
    return pl.pallas_call(
        body,
        out_shape=outs,
        in_specs=ins,
        out_specs=[VMEM] * len(outs),
        scratch_shapes=scratch,
        compiler_params=pltpu.CompilerParams(vmem_limit_bytes=mib * MIB),
        cost_estimate=pl.CostEstimate(flops=flops, bytes_accessed=nbytes, transcendentals=0),
    )


def shards(tokens, counts, neighbours, side_keys, cross_qkv, cross_out, time_qkv, time_out):
    cam_here, frames_here, token_count, model = tokens.shape
    cameras = cam_here * lax.axis_size("cam")
    frames = lax.axis_size("frame")
    rows = cam_here * token_count
    bf16 = jnp.bfloat16
    spread = functools.partial(jax.ShapeDtypeStruct, dtype=bf16)

    flat = tokens.reshape(rows, model)
    cross_t, time_t = cross_qkv.T, time_qkv.T
    side = jnp.pad(side_keys.astype(jnp.float32), ((0, 0), (0, KEY_LANES - INNER)))

    first, second = kernel_call(
        norm_kernel, [VMEM], [spread((token_count, model))] * 2, [], 16, 5_000_000, 2_400_000
    )(flat)
    lower = passed_along(second, "cam", 1)
    upper = passed_along(first, "cam", -1)
    lower_counts = passed_along(counts, "cam", 1)
    upper_counts = passed_along(counts, "cam", -1)

    query, part = kernel_call(
        functools.partial(local_kernel, cameras),
        [SMEM, SMEM, VMEM, VMEM, VMEM, VMEM],
        [
            jax.ShapeDtypeStruct((INNER, rows), jnp.float32),
            jax.ShapeDtypeStruct((2, HEADS, HEAD + 8, token_count), jnp.float32),
        ],
        [pltpu.VMEM((INNER, rows), jnp.float32)],
        32,
        6_000_000_000,
        20_000_000,
    )(counts, neighbours, first, second, cross_t, side)

    mixed, payload = kernel_call(
        functools.partial(merge_kernel, cameras),
        [SMEM] * 4 + [VMEM] * 8,
        [spread((rows, model)), spread((rows, model + LANES))],
        [pltpu.VMEM((INNER, rows), jnp.float32)],
        32,
        4_000_000_000,
        12_000_000,
    )(counts, lower_counts, upper_counts, neighbours, flat, lower, upper, cross_t, side, query, part, cross_out)

    chunk = rows // frames
    arrived = lax.all_to_all(
        payload.reshape(frames, chunk, model + LANES), "frame", split_axis=0, concat_axis=0, tiled=True
    )
    (attended,) = kernel_call(
        functools.partial(time_kernel, frames),
        [VMEM] * 2,
        [spread((rows, INNER))],
        [pltpu.VMEM((INNER, rows), jnp.float32)] * 2,
        32,
        6_000_000_000,
        10_000_000,
    )(arrived.reshape(rows, model + LANES), time_t)
    returned = lax.all_to_all(
        attended.reshape(frames, chunk, INNER), "frame", split_axis=0, concat_axis=0, tiled=True
    )
    (out,) = kernel_call(
        final_kernel,
        [VMEM] * 3,
        [spread((rows, model))],
        [],
        32,
        700_000_000,
        4_000_000,
    )(returned.reshape(rows, INNER), time_out, mixed)
    return out.reshape(tokens.shape)


def solution(mesh):
    return jax.shard_map(
        shards,
        mesh=mesh,
        in_specs=(
            P("cam", "frame", None, None),
            P("cam", "frame"),
            P("cam", None),
            P(),
            P(),
            P(),
            P(),
            P(),
        ),
        out_specs=P("cam", "frame", None, None),
        check_vma=False,
    )
```

```python
import functools
import math

import jax
import jax.numpy as jnp
from jax import lax
from jax.experimental import pallas as pl
from jax.experimental.pallas import tpu as pltpu
from jax.sharding import PartitionSpec as P

HEADS = 8
HEAD = 72
INNER = HEADS * HEAD
EPS = 1e-06
ROW_TOKENS = 64
BIG = 1e30
COEF = HEAD ** (-0.5) * math.log2(math.e)
LANES = 128
KEY_LANES = 640
MIB = 1 << 20


def to_owners(x):
    return lax.all_to_all(x, "frame", split_axis=0, concat_axis=0, tiled=True)


def cam_is_odd():
    return lax.rem(lax.axis_index("cam"), 2)


def exchange_pairs(peers):
    inside, early, late = [], [], []
    for i in range(0, peers, 2):
        inside += [(i, i + 1), (i + 1, i)]
        last = (i + peers - 1) % peers
        (late if (i // 2) % 2 else early).extend([(last, i), (i, last)])
    return inside, early, late


def is_early():
    peers = lax.axis_size("cam")
    return lax.rem(lax.rem(lax.axis_index("cam") + 1, peers) // 2, 2) == 0


def dot_nt(a, b):
    return lax.dot_general(a, b, (((1,), (1,)), ((), ())), preferred_element_type=jnp.float32)


def dot_nn(a, b):
    return lax.dot_general(a, b, (((1,), (0,)), ((), ())), preferred_element_type=jnp.float32)


def normalize(values):
    values = values.astype(jnp.float32)
    mean = jnp.mean(values, axis=-1, keepdims=True)
    centred = values - mean
    variance = jnp.mean(centred * centred, axis=-1, keepdims=True)
    return (centred * lax.rsqrt(variance + EPS)).astype(jnp.bfloat16)


def keys_bias(rows, count):
    position = lax.broadcasted_iota(jnp.int32, (rows, LANES), 0).astype(jnp.float32)
    return jnp.where(position < ROW_TOKENS * count, 0.0, -BIG).astype(jnp.bfloat16)


def key_window(keys, head, bias):
    window = keys[:, head * HEAD : head * HEAD + LANES]
    lane = lax.broadcasted_iota(jnp.int32, window.shape, 1)
    window = jnp.where(lane < HEAD, window, jnp.zeros_like(window))
    return window if bias is None else jnp.where(lane == HEAD, bias, window)


def one_then_zeros(rows, columns):
    return jnp.where(lax.broadcasted_iota(jnp.int32, (rows, columns), 0) == 0, 1.0, 0.0)


def head_rows(x, head):
    return x[head * HEAD : (head + 1) * HEAD, :]


def rounded(x):
    return x.astype(jnp.bfloat16).astype(jnp.float32)


def padded_keys(keys):
    fill = jnp.zeros((keys.shape[0], KEY_LANES - keys.shape[1]), jnp.float32)
    return jnp.concatenate([keys, fill], axis=1).astype(jnp.bfloat16)


def with_side(keys, side):
    return (keys.astype(jnp.float32) + side).astype(jnp.bfloat16)


def side_row(side, neighbours_ref, cam, lower, cameras, cam_here):
    camera = lax.axis_index("cam") * cam_here + cam
    first_lower = neighbours_ref[cam, 0] == lax.rem(camera + cameras - 1, cameras)
    pick_first = first_lower if lower else jnp.logical_not(first_lower)
    return jnp.where(pick_first, side[0:1, :], side[1:2, :])


def staggered(items, score, rest, ahead):
    scores = [score(item) for item in items[:ahead]]
    for i, item in enumerate(items):
        if i + ahead < len(items):
            scores.append(score(items[i + ahead]))
        rest(item, scores[i])
        scores[i] = None


def norm_kernel(counts_ref, tokens_ref, across_ref, inside_ref, normed_ref):
    rows = normed_ref.shape[0] // 2
    odd = cam_is_odd()
    for cam, out_ref in ((odd, across_ref), (1 - odd, inside_ref)):
        here = pl.ds(pl.multiple_of(cam * rows, rows), rows)
        normed = normalize(tokens_ref[here, :])
        out_ref[:rows, :] = normed
        count = counts_ref[0, cam].astype(jnp.float32)
        out_ref[rows:, :] = jnp.full((out_ref.shape[0] - rows, out_ref.shape[1]), count, jnp.float32).astype(jnp.bfloat16)
        normed_ref[here, :] = normed


def local_kernel(
    cameras, counts_ref, neighbours_ref, normed_ref, weight_ref, side_ref, query_ref, part_ref, info_ref, value_ref
):
    rows = normed_ref.shape[0] // 2
    normed = normed_ref[...]
    keys = padded_keys(dot_nt(normed, weight_ref[INNER : 2 * INNER, :]))
    query_ref[...] = rounded(dot_nt(weight_ref[:INNER, :], normed))
    value_ref[...] = rounded(dot_nt(weight_ref[2 * INNER :, :], normed))
    sides = jnp.concatenate(
        [side_ref[...].astype(jnp.float32), jnp.zeros((2, KEY_LANES - INNER), jnp.float32)], axis=1
    )
    counts = [counts_ref[0, c].astype(jnp.float32) for c in range(2)]
    for c in range(2):
        info_ref[c : c + 1, :] = side_row(sides, neighbours_ref, c, c == 0, cameras, 2)
        info_ref[2 + c : 3 + c, :] = jnp.full((1, KEY_LANES), counts[c], jnp.float32)
    info_ref[4:, :] = jnp.zeros((info_ref.shape[0] - 4, KEY_LANES), jnp.float32)
    biases = [keys_bias(rows, counts[c]) for c in range(2)]
    one_rows = one_then_zeros(LANES - HEAD, rows)
    value_ones = one_then_zeros(8, 2 * rows)
    kept = []
    for c in range(2):
        own, other = slice(c * rows, (c + 1) * rows), slice((1 - c) * rows, (2 - c) * rows)
        side = side_row(sides, neighbours_ref, c, c == 1, cameras, 2)
        kept.append(
            (
                own,
                other,
                jnp.concatenate([keys[own], with_side(keys[other], side)], axis=0),
                jnp.concatenate([biases[c], biases[1 - c]], axis=0),
            )
        )

    def score(item):
        c, h = item
        own, _, k_all, bias = kept[c]
        q = jnp.concatenate([head_rows(query_ref[:, own], h), one_rows], axis=0).astype(jnp.bfloat16)
        return dot_nn(key_window(k_all, h, bias), q)

    def rest(item, scores):
        c, h = item
        own, other, _, _ = kept[c]
        highest = jnp.max(scores, axis=0, keepdims=True)
        expo = jnp.exp2((scores - highest) * COEF).astype(jnp.bfloat16)
        v = jnp.concatenate([head_rows(value_ref[:, own], h), head_rows(value_ref[:, other], h)], axis=1)
        summed = dot_nn(jnp.concatenate([v, value_ones], axis=0).astype(jnp.bfloat16), expo)
        row = lax.broadcasted_iota(jnp.int32, summed.shape, 0)
        part_ref[c, h] = jnp.where(row == HEAD + 1, highest, summed)

    staggered([(c, h) for c in range(2) for h in range(HEADS)], score, rest, 3)


def merge_kernel(
    early_ref, late_ref, inside_ref, weight_ref, info_ref, query_ref, part_ref, tokens_ref, out_weight_ref, mixed_ref,
    payload_ref, far_ref, value_ref,
):
    rows = tokens_ref.shape[0] // 2
    model = tokens_ref.shape[1]
    odd, early = cam_is_odd(), is_early()
    far_ref[pl.ds(pl.multiple_of(odd * rows, rows), rows), :] = jnp.where(early, early_ref[:rows, :], late_ref[:rows, :])
    far_ref[pl.ds(pl.multiple_of((1 - odd) * rows, rows), rows), :] = inside_ref[:rows, :]
    across_count = jnp.where(early, early_ref[rows : rows + 16, :LANES], late_ref[rows : rows + 16, :LANES])
    inside_count = inside_ref[rows : rows + 16, :LANES]
    even = odd == 0
    far_counts = (jnp.where(even, across_count, inside_count), jnp.where(even, inside_count, across_count))
    far = far_ref[...]
    keys = padded_keys(dot_nt(far, weight_ref[INNER : 2 * INNER, :]))
    value_ref[...] = rounded(dot_nt(weight_ref[2 * INNER :, :], far))
    one_rows = one_then_zeros(LANES - HEAD, rows)
    value_ones = one_then_zeros(8, rows)
    kept = []
    for c in range(2):
        here = slice(c * rows, (c + 1) * rows)
        bias = keys_bias(rows, far_counts[c].astype(jnp.float32)[:1, :])
        kept.append((here, with_side(keys[here], info_ref[c : c + 1, :]), bias))
    pieces = [[], []]

    def score(item):
        c, h = item
        here, k_all, bias = kept[c]
        q = jnp.concatenate([head_rows(query_ref[:, here], h), one_rows], axis=0).astype(jnp.bfloat16)
        return dot_nn(key_window(k_all, h, bias), q)

    def rest(item, scores):
        c, h = item
        here = kept[c][0]
        part = part_ref[c, h]
        before = part[HEAD + 1 : HEAD + 2, :]
        highest = jnp.maximum(jnp.max(scores, axis=0, keepdims=True), before)
        expo = jnp.exp2((scores - highest) * COEF).astype(jnp.bfloat16)
        v = jnp.concatenate([head_rows(value_ref[:, here], h), value_ones], axis=0).astype(jnp.bfloat16)
        summed = part * jnp.exp2((before - highest) * COEF) + dot_nn(v, expo)
        pieces[c].append(summed[:HEAD] * (1.0 / summed[HEAD : HEAD + 1]))

    staggered([(c, h) for c in range(2) for h in range(HEADS)], score, rest, 3)
    for c in range(2):
        here = slice(c * rows, (c + 1) * rows)
        attended = jnp.concatenate(pieces[c], axis=0).T.astype(jnp.bfloat16)
        mixed = dot_nn(attended, out_weight_ref[...]) + tokens_ref[here, :].astype(jnp.float32)
        mixed = mixed.astype(jnp.bfloat16)
        mixed_ref[here, :] = mixed
        width = mixed.shape[1]
        payload_ref[here, :width] = normalize(mixed)
        position = lax.broadcasted_iota(jnp.int32, (rows, LANES), 0).astype(jnp.float32)
        valid = position < ROW_TOKENS * info_ref[2 + c : 3 + c, :LANES]
        payload_ref[here, width:] = jnp.where(valid, 1.0, 0.0).astype(jnp.bfloat16)


def time_kernel(frames, payload_ref, weight_ref, out_ref, query_ref, value_ref):
    rows = payload_ref.shape[0]
    places = rows // frames
    model = weight_ref.shape[1]
    normed = payload_ref[:, :model]
    keys = padded_keys(dot_nt(normed, weight_ref[INNER : 2 * INNER, :]))
    query_ref[...] = rounded(dot_nt(weight_ref[:INNER, :], normed))
    value_ref[...] = rounded(dot_nt(weight_ref[2 * INNER :, :], normed))
    lane = lax.broadcasted_iota(jnp.int32, (rows, LANES), 1)
    key = lax.broadcasted_iota(jnp.int32, (rows, LANES), 0)
    invalid = payload_ref[:, model:].astype(jnp.float32) < 0.5
    key_mask = jnp.where(
        lane < frames,
        jnp.where(jnp.logical_and(invalid, lane != key // places), -BIG, 0.0),
        jnp.where(lane - frames == key % places, 1.0, 0.0),
    ).astype(jnp.bfloat16)
    entry = lax.broadcasted_iota(jnp.int32, (LANES, rows), 0)
    query = lax.broadcasted_iota(jnp.int32, (LANES, rows), 1)
    query_mask = jnp.where(
        entry < frames,
        jnp.where(entry == query // places, 1.0, 0.0),
        jnp.where(jnp.logical_and(entry < frames + places, entry - frames != query % places), -BIG, 0.0),
    ).astype(jnp.bfloat16)
    zero_rows = jnp.zeros((LANES - HEAD, rows), jnp.float32)
    value_ones = one_then_zeros(8, rows)
    block = 256
    blocks = rows // block
    pieces = [[] for _ in range(blocks)]

    def score(item):
        h, b = item
        here = slice(b * block, (b + 1) * block)
        q = jnp.concatenate([head_rows(query_ref[:, here], h), zero_rows[:, here]], axis=0).astype(jnp.bfloat16)
        return dot_nn(
            jnp.concatenate([key_window(keys, h, None), key_mask], axis=1),
            jnp.concatenate([q, query_mask[:, here]], axis=0),
        )

    def rest(item, scores):
        h, b = item
        highest = jnp.max(scores, axis=0, keepdims=True)
        expo = jnp.exp2((scores - highest) * COEF).astype(jnp.bfloat16)
        v = jnp.concatenate([head_rows(value_ref[...], h), value_ones], axis=0).astype(jnp.bfloat16)
        summed = dot_nn(v, expo)
        pieces[b].append(summed[:HEAD] * (1.0 / summed[HEAD : HEAD + 1]))

    staggered([(h, b) for h in range(HEADS) for b in range(blocks)], score, rest, 3)
    for b in range(blocks):
        out_ref[b * block : (b + 1) * block, :] = jnp.concatenate(pieces[b], axis=0).T.astype(jnp.bfloat16)


def final_kernel(attended_ref, weight_ref, mixed_ref, out_ref):
    result = dot_nn(attended_ref[...], weight_ref[...]) + mixed_ref[...].astype(jnp.float32)
    out_ref[...] = result.astype(jnp.bfloat16)


SMEM = pl.BlockSpec(memory_space=pltpu.SMEM)
VMEM = pl.BlockSpec(memory_space=pltpu.VMEM)


def kernel_call(body, ins, outs, scratch, mib, flops, nbytes):
    return pl.pallas_call(
        body,
        out_shape=outs,
        in_specs=ins,
        out_specs=[VMEM] * len(outs),
        scratch_shapes=scratch,
        compiler_params=pltpu.CompilerParams(vmem_limit_bytes=mib * MIB),
        cost_estimate=pl.CostEstimate(flops=flops, bytes_accessed=nbytes, transcendentals=0),
    )


def shards(tokens, counts, neighbours, side_keys, cross_qkv, cross_out, time_qkv, time_out):
    cam_here, frames_here, token_count, model = tokens.shape
    cameras = cam_here * lax.axis_size("cam")
    frames = lax.axis_size("frame")
    rows = cam_here * token_count
    bf16 = jnp.bfloat16
    spread = functools.partial(jax.ShapeDtypeStruct, dtype=bf16)

    flat = tokens.reshape(rows, model)
    own_counts = counts.reshape(1, cam_here)
    cross_t, time_t = cross_qkv.T, time_qkv.T
    inside_pairs, early_pairs, late_pairs = exchange_pairs(lax.axis_size("cam"))
    sent = token_count + 16

    across, inside, normed = kernel_call(
        norm_kernel,
        [SMEM, VMEM],
        [spread((sent, model))] * 2 + [spread((rows, model))],
        [],
        16,
        6_000_000_000,
        2_400_000,
    )(own_counts, flat)
    early_far = lax.ppermute(across, "cam", early_pairs)
    inside_far = lax.ppermute(inside, "cam", inside_pairs)

    query, part, info = kernel_call(
        functools.partial(local_kernel, cameras),
        [SMEM, SMEM, VMEM, VMEM, VMEM],
        [
            jax.ShapeDtypeStruct((INNER, rows), jnp.float32),
            jax.ShapeDtypeStruct((2, HEADS, HEAD + 8, token_count), jnp.float32),
            jax.ShapeDtypeStruct((8, KEY_LANES), jnp.float32),
        ],
        [pltpu.VMEM((INNER, rows), jnp.float32)],
        32,
        6_000_000_000,
        20_000_000,
    )(own_counts, neighbours, normed, cross_t, side_keys)
    across, query = lax.optimization_barrier((across, query))
    late_far = lax.ppermute(across, "cam", late_pairs)

    mixed, payload = kernel_call(
        merge_kernel,
        [VMEM] * 9,
        [spread((rows, model)), spread((rows, model + LANES))],
        [pltpu.VMEM((rows, model), bf16), pltpu.VMEM((INNER, rows), jnp.float32)],
        32,
        4_000_000_000,
        12_000_000,
    )(early_far, late_far, inside_far, cross_t, info, query, part, flat, cross_out)

    chunk = rows // frames
    arrived = to_owners(payload.reshape(frames, chunk, model + LANES))
    (attended,) = kernel_call(
        functools.partial(time_kernel, frames),
        [VMEM] * 2,
        [spread((rows, INNER))],
        [pltpu.VMEM((INNER, rows), jnp.float32)] * 2,
        32,
        6_000_000_000,
        10_000_000,
    )(arrived.reshape(rows, model + LANES), time_t)
    returned = to_owners(attended.reshape(frames, chunk, INNER))
    (out,) = kernel_call(
        final_kernel,
        [VMEM] * 3,
        [spread((rows, model))],
        [],
        32,
        700_000_000,
        4_000_000,
    )(returned.reshape(rows, INNER), time_out, mixed)
    return out.reshape(tokens.shape)


def solution(mesh):
    return jax.shard_map(
        shards,
        mesh=mesh,
        in_specs=(
            P("cam", "frame", None, None),
            P("cam", "frame"),
            P("cam", None),
            P(),
            P(),
            P(),
            P(),
            P(),
        ),
        out_specs=P("cam", "frame", None, None),
        check_vma=False,
    )
```

```python
import functools
import math

import jax
import jax.numpy as jnp
from jax import lax
from jax.experimental import pallas as pl
from jax.experimental.pallas import tpu as pltpu
from jax.sharding import PartitionSpec as P

HEADS = 8
HEAD = 72
INNER = HEADS * HEAD
EPS = 1e-06
ROW_TOKENS = 64
BIG = 1e30
COEF = HEAD ** (-0.5) * math.log2(math.e)
LANES = 128
KEY_LANES = 640
MIB = 1 << 20


def to_owners(x):
    return lax.all_to_all(x, "frame", split_axis=0, concat_axis=0, tiled=True)


def cam_is_odd():
    return lax.rem(lax.axis_index("cam"), 2)


def exchange_pairs(peers):
    inside, early, late = [], [], []
    for i in range(0, peers, 2):
        inside += [(i, i + 1), (i + 1, i)]
        last = (i + peers - 1) % peers
        (late if (i // 2) % 2 else early).extend([(last, i), (i, last)])
    return inside, early, late


def is_early():
    peers = lax.axis_size("cam")
    return lax.rem(lax.rem(lax.axis_index("cam") + 1, peers) // 2, 2) == 0


def dot_nt(a, b):
    return lax.dot_general(a, b, (((1,), (1,)), ((), ())), preferred_element_type=jnp.float32)


def dot_nn(a, b):
    return lax.dot_general(a, b, (((1,), (0,)), ((), ())), preferred_element_type=jnp.float32)


def normalize(values):
    values = values.astype(jnp.float32)
    mean = jnp.mean(values, axis=-1, keepdims=True)
    centred = values - mean
    variance = jnp.mean(centred * centred, axis=-1, keepdims=True)
    return (centred * lax.rsqrt(variance + EPS)).astype(jnp.bfloat16)


def keys_bias(rows, count):
    position = lax.broadcasted_iota(jnp.int32, (rows, LANES), 0).astype(jnp.float32)
    return jnp.where(position < ROW_TOKENS * count, 0.0, -BIG).astype(jnp.bfloat16)


def key_window(keys, head, bias):
    window = keys[:, head * HEAD : head * HEAD + LANES]
    lane = lax.broadcasted_iota(jnp.int32, window.shape, 1)
    window = jnp.where(lane < HEAD, window, jnp.zeros_like(window))
    return window if bias is None else jnp.where(lane == HEAD, bias, window)


def one_then_zeros(rows, columns):
    return jnp.where(lax.broadcasted_iota(jnp.int32, (rows, columns), 0) == 0, 1.0, 0.0)


def head_rows(x, head):
    return x[head * HEAD : (head + 1) * HEAD, :]


def rounded(x):
    return x.astype(jnp.bfloat16).astype(jnp.float32)


def padded_keys(keys):
    fill = jnp.zeros((keys.shape[0], KEY_LANES - keys.shape[1]), jnp.float32)
    return jnp.concatenate([keys, fill], axis=1).astype(jnp.bfloat16)


def with_side(keys, side):
    return (keys.astype(jnp.float32) + side).astype(jnp.bfloat16)


def side_row(side, neighbours_ref, cam, lower, cameras, cam_here):
    camera = lax.axis_index("cam") * cam_here + cam
    first_lower = neighbours_ref[cam, 0] == lax.rem(camera + cameras - 1, cameras)
    return jnp.where(first_lower == lower, side[0:1, :], side[1:2, :])


def staggered(items, score, rest, ahead):
    scores = [score(item) for item in items[:ahead]]
    for i, item in enumerate(items):
        if i + ahead < len(items):
            scores.append(score(items[i + ahead]))
        rest(item, scores[i])
        scores[i] = None


def camera_rows(cam, rows):
    return pl.ds(pl.multiple_of(cam * rows, rows), rows)


def norm_kernel(counts_ref, tokens_ref, outer_ref, inner_ref):
    rows = tokens_ref.shape[0] // 2
    odd = cam_is_odd()
    for cam, out_ref in ((odd, outer_ref), (1 - odd, inner_ref)):
        out_ref[:rows, :] = normalize(tokens_ref[camera_rows(cam, rows), :])
        count = counts_ref[0, cam].astype(jnp.float32)
        out_ref[rows:, :] = jnp.full((out_ref.shape[0] - rows, out_ref.shape[1]), count, jnp.float32).astype(jnp.bfloat16)


def write_finished(i, pieces, tokens, out_weight_ref, info_ref, mixed_ref, payload_ref):
    attended = jnp.concatenate(pieces, axis=0).T.astype(jnp.bfloat16)
    mixed = (dot_nn(attended, out_weight_ref[...]) + tokens.astype(jnp.float32)).astype(jnp.bfloat16)
    rows, width = mixed.shape
    mixed_ref[...] = mixed
    payload_ref[:rows, :width] = normalize(mixed)
    position = lax.broadcasted_iota(jnp.int32, (rows, LANES), 0).astype(jnp.float32)
    valid = position < ROW_TOKENS * info_ref[2 + i : 3 + i, :LANES]
    payload_ref[:rows, width:] = jnp.where(valid, 1.0, 0.0).astype(jnp.bfloat16)


def local_kernel(
    cameras, counts_ref, neighbours_ref, outer_ref, inner_ref, far_ref, weight_ref, side_ref, tokens_ref, out_weight_ref,
    query_ref, part_ref, info_ref, mixed_ref, payload_ref, value_ref,
):
    rows = mixed_ref.shape[0]
    odd = cam_is_odd()
    cams = (odd, 1 - odd)
    normed = jnp.concatenate([outer_ref[:rows, :], inner_ref[:rows, :], far_ref[:rows, :]], axis=0)
    keys = padded_keys(dot_nt(normed, weight_ref[INNER : 2 * INNER, :]))
    query_ref[...] = rounded(dot_nt(weight_ref[:INNER, :], normed[: 2 * rows]))
    value_ref[...] = rounded(dot_nt(weight_ref[2 * INNER :, :], normed))
    sides = jnp.concatenate(
        [side_ref[...].astype(jnp.float32), jnp.zeros((2, KEY_LANES - INNER), jnp.float32)], axis=1
    )
    far_sides = [side_row(sides, neighbours_ref, cam, cam == 0, cameras, 2) for cam in cams]
    near_sides = [side_row(sides, neighbours_ref, cam, cam == 1, cameras, 2) for cam in cams]
    counts = [counts_ref[0, cam].astype(jnp.float32) for cam in cams]
    info_ref[0:1, :] = far_sides[0]
    info_ref[1:2, :] = far_sides[1]
    for i in range(2):
        info_ref[2 + i : 3 + i, :] = jnp.full((1, KEY_LANES), counts[i], jnp.float32)
    info_ref[4:, :] = jnp.zeros((info_ref.shape[0] - 4, KEY_LANES), jnp.float32)
    biases = [keys_bias(rows, count) for count in counts]
    far_bias = keys_bias(rows, far_ref[rows : rows + 16, :LANES].astype(jnp.float32)[:1])
    one_rows = one_then_zeros(LANES - HEAD, rows)
    value_ones = one_then_zeros(8, 3 * rows)
    outer, inner, far = (slice(i * rows, (i + 1) * rows) for i in range(3))
    kept = (
        (
            outer,
            (outer, inner),
            jnp.concatenate([keys[outer], with_side(keys[inner], near_sides[0])], axis=0),
            jnp.concatenate([biases[0], biases[1]], axis=0),
        ),
        (
            inner,
            (inner, outer, far),
            jnp.concatenate(
                [keys[inner], with_side(keys[outer], near_sides[1]), with_side(keys[far], far_sides[1])], axis=0
            ),
            jnp.concatenate([biases[1], biases[0], far_bias], axis=0),
        ),
    )
    pieces = []

    def score(item):
        i, h = item
        own, _, k_all, bias = kept[i]
        q = jnp.concatenate([head_rows(query_ref[:, own], h), one_rows], axis=0).astype(jnp.bfloat16)
        return dot_nn(key_window(k_all, h, bias), q)

    def rest(item, scores):
        i, h = item
        blocks = kept[i][1]
        highest = jnp.max(scores, axis=0, keepdims=True)
        expo = jnp.exp2((scores - highest) * COEF).astype(jnp.bfloat16)
        v = jnp.concatenate([head_rows(value_ref[:, block], h) for block in blocks], axis=1)
        v = jnp.concatenate([v, value_ones[:, : v.shape[1]]], axis=0).astype(jnp.bfloat16)
        summed = dot_nn(v, expo)
        if i == 0:
            row = lax.broadcasted_iota(jnp.int32, summed.shape, 0)
            part_ref[h] = jnp.where(row == HEAD + 1, highest, summed)
        else:
            pieces.append(summed[:HEAD] * (1.0 / summed[HEAD : HEAD + 1]))

    staggered([(i, h) for i in (1, 0) for h in range(HEADS)], score, rest, 3)
    tokens = tokens_ref[camera_rows(1 - odd, rows), :]
    write_finished(1, pieces, tokens, out_weight_ref, info_ref, mixed_ref, payload_ref)


def outer_kernel(
    early_ref, late_ref, weight_ref, info_ref, query_ref, part_ref, tokens_ref, out_weight_ref, inner_ref, mixed_ref,
    payload_ref, value_ref,
):
    rows = mixed_ref.shape[0]
    early = is_early()
    far = jnp.where(early, early_ref[:rows, :], late_ref[:rows, :])
    far_count = jnp.where(early, early_ref[rows : rows + 16, :LANES], late_ref[rows : rows + 16, :LANES])
    keys = padded_keys(dot_nt(far, weight_ref[INNER : 2 * INNER, :]))
    keys = with_side(keys, info_ref[0:1, :])
    value_ref[...] = rounded(dot_nt(weight_ref[2 * INNER :, :], far))
    payload_ref[rows:, :] = inner_ref[...]
    bias = keys_bias(rows, far_count.astype(jnp.float32)[:1])
    one_rows = one_then_zeros(LANES - HEAD, rows)
    value_ones = one_then_zeros(8, rows)
    pieces = []

    def score(h):
        q = jnp.concatenate([head_rows(query_ref[:, :rows], h), one_rows], axis=0).astype(jnp.bfloat16)
        return dot_nn(key_window(keys, h, bias), q)

    def rest(h, scores):
        part = part_ref[h]
        before = part[HEAD + 1 : HEAD + 2, :]
        highest = jnp.maximum(jnp.max(scores, axis=0, keepdims=True), before)
        expo = jnp.exp2((scores - highest) * COEF).astype(jnp.bfloat16)
        v = jnp.concatenate([head_rows(value_ref[...], h), value_ones], axis=0).astype(jnp.bfloat16)
        summed = part * jnp.exp2((before - highest) * COEF) + dot_nn(v, expo)
        pieces.append(summed[:HEAD] * (1.0 / summed[HEAD : HEAD + 1]))

    staggered(list(range(HEADS)), score, rest, 3)
    tokens = tokens_ref[camera_rows(cam_is_odd(), rows), :]
    write_finished(0, pieces, tokens, out_weight_ref, info_ref, mixed_ref, payload_ref)


def time_kernel(frames, payload_ref, weight_ref, out_ref, query_ref, value_ref):
    rows = payload_ref.shape[0]
    places = rows // frames
    model = weight_ref.shape[1]
    normed = payload_ref[:, :model]
    keys = padded_keys(dot_nt(normed, weight_ref[INNER : 2 * INNER, :]))
    query_ref[...] = rounded(dot_nt(weight_ref[:INNER, :], normed))
    value_ref[...] = rounded(dot_nt(weight_ref[2 * INNER :, :], normed))
    lane = lax.broadcasted_iota(jnp.int32, (rows, LANES), 1)
    key = lax.broadcasted_iota(jnp.int32, (rows, LANES), 0)
    invalid = payload_ref[:, model:].astype(jnp.float32) < 0.5
    key_mask = jnp.where(
        lane < frames,
        jnp.where(jnp.logical_and(invalid, lane != key // places), -BIG, 0.0),
        jnp.where(lane - frames == key % places, 1.0, 0.0),
    ).astype(jnp.bfloat16)
    entry = lax.broadcasted_iota(jnp.int32, (LANES, rows), 0)
    query = lax.broadcasted_iota(jnp.int32, (LANES, rows), 1)
    query_mask = jnp.where(
        entry < frames,
        jnp.where(entry == query // places, 1.0, 0.0),
        jnp.where(jnp.logical_and(entry < frames + places, entry - frames != query % places), -BIG, 0.0),
    ).astype(jnp.bfloat16)
    zero_rows = jnp.zeros((LANES - HEAD, rows), jnp.float32)
    value_ones = one_then_zeros(8, rows)
    block = 256
    blocks = rows // block
    pieces = [[] for _ in range(blocks)]

    def score(item):
        h, b = item
        here = slice(b * block, (b + 1) * block)
        q = jnp.concatenate([head_rows(query_ref[:, here], h), zero_rows[:, here]], axis=0).astype(jnp.bfloat16)
        return dot_nn(
            jnp.concatenate([key_window(keys, h, None), key_mask], axis=1),
            jnp.concatenate([q, query_mask[:, here]], axis=0),
        )

    def rest(item, scores):
        h, b = item
        highest = jnp.max(scores, axis=0, keepdims=True)
        expo = jnp.exp2((scores - highest) * COEF).astype(jnp.bfloat16)
        v = jnp.concatenate([head_rows(value_ref[...], h), value_ones], axis=0).astype(jnp.bfloat16)
        summed = dot_nn(v, expo)
        pieces[b].append(summed[:HEAD] * (1.0 / summed[HEAD : HEAD + 1]))

    staggered([(h, b) for h in range(HEADS) for b in range(blocks)], score, rest, 3)
    for b in range(blocks):
        out_ref[b * block : (b + 1) * block, :] = jnp.concatenate(pieces[b], axis=0).T.astype(jnp.bfloat16)


def final_kernel(attended_ref, weight_ref, outer_ref, inner_ref, out_hbm, block_ref, sems):
    rows = outer_ref.shape[0]
    size = block_ref.shape[1]
    odd = cam_is_odd()
    copies = []
    for i, (cam, mixed_ref) in enumerate(((odd, outer_ref), (1 - odd, inner_ref))):
        for start in range(0, rows, size):
            slot = len(copies)
            result = dot_nn(attended_ref[i * rows + start : i * rows + start + size, :], weight_ref[...])
            result = result + mixed_ref[start : start + size, :].astype(jnp.float32)
            block_ref[slot] = result.astype(jnp.bfloat16)
            there = pl.ds(pl.multiple_of(cam * rows + start, size), size)
            copies.append(pltpu.make_async_copy(block_ref.at[slot], out_hbm.at[there], sems.at[slot]))
            copies[-1].start()
    for copy in copies:
        copy.wait()


SMEM = pl.BlockSpec(memory_space=pltpu.SMEM)
VMEM = pl.BlockSpec(memory_space=pltpu.VMEM)
ANY = pl.BlockSpec(memory_space=pl.ANY)


def kernel_call(body, ins, outs, scratch, mib, flops, nbytes, out_space=VMEM):
    return pl.pallas_call(
        body,
        out_shape=outs,
        in_specs=ins,
        out_specs=[out_space] * len(outs),
        scratch_shapes=scratch,
        compiler_params=pltpu.CompilerParams(vmem_limit_bytes=mib * MIB),
        cost_estimate=pl.CostEstimate(flops=flops, bytes_accessed=nbytes, transcendentals=0),
    )


def shards(tokens, counts, neighbours, side_keys, cross_qkv, cross_out, time_qkv, time_out):
    cam_here, frames_here, token_count, model = tokens.shape
    cameras = cam_here * lax.axis_size("cam")
    frames = lax.axis_size("frame")
    rows = cam_here * token_count
    bf16 = jnp.bfloat16
    spread = functools.partial(jax.ShapeDtypeStruct, dtype=bf16)

    flat = tokens.reshape(rows, model)
    own_counts = counts.reshape(1, cam_here)
    cross_t, time_t = cross_qkv.T, time_qkv.T
    inside_pairs, early_pairs, late_pairs = exchange_pairs(lax.axis_size("cam"))
    sent = token_count + 16

    outer, inner = kernel_call(
        norm_kernel, [SMEM, VMEM], [spread((sent, model))] * 2, [], 16, 6_000_000_000, 2_400_000
    )(own_counts, flat)
    early_far = lax.ppermute(outer, "cam", early_pairs)
    inner_far = lax.ppermute(inner, "cam", inside_pairs)

    query, part, info, mixed_inner, payload_inner = kernel_call(
        functools.partial(local_kernel, cameras),
        [SMEM, SMEM] + [VMEM] * 7,
        [
            jax.ShapeDtypeStruct((INNER, rows), jnp.float32),
            jax.ShapeDtypeStruct((HEADS, HEAD + 8, token_count), jnp.float32),
            jax.ShapeDtypeStruct((8, KEY_LANES), jnp.float32),
            spread((token_count, model)),
            spread((token_count, model + LANES)),
        ],
        [pltpu.VMEM((INNER, rows + token_count), jnp.float32)],
        36,
        8_000_000_000,
        20_000_000,
    )(own_counts, neighbours, outer, inner, inner_far, cross_t, side_keys, flat, cross_out)
    outer, payload_inner = lax.optimization_barrier((outer, payload_inner))
    late_far = lax.ppermute(outer, "cam", late_pairs)
    mixed_outer, payload = kernel_call(
        outer_kernel,
        [VMEM] * 9,
        [spread((token_count, model)), spread((rows, model + LANES))],
        [pltpu.VMEM((INNER, token_count), jnp.float32)],
        32,
        2_500_000_000,
        8_000_000,
    )(early_far, late_far, cross_t, info, query, part, flat, cross_out, payload_inner)

    chunk = rows // frames
    arrived = to_owners(payload.reshape(frames, chunk, model + LANES))
    (attended,) = kernel_call(
        functools.partial(time_kernel, frames),
        [VMEM] * 2,
        [spread((rows, INNER))],
        [pltpu.VMEM((INNER, rows), jnp.float32)] * 2,
        32,
        6_000_000_000,
        10_000_000,
    )(arrived.reshape(rows, model + LANES), time_t)
    returned = to_owners(attended.reshape(frames, chunk, INNER))
    (out,) = kernel_call(
        final_kernel,
        [VMEM] * 4,
        [spread((rows, model))],
        [pltpu.VMEM((4, rows // 4, model), bf16), pltpu.SemaphoreType.DMA((4,))],
        32,
        700_000_000,
        4_000_000,
        ANY,
    )(returned.reshape(rows, INNER), time_out, mixed_outer, mixed_inner)
    return out.reshape(tokens.shape)


def solution(mesh):
    return jax.shard_map(
        shards,
        mesh=mesh,
        in_specs=(
            P("cam", "frame", None, None),
            P("cam", "frame"),
            P("cam", None),
            P(),
            P(),
            P(),
            P(),
            P(),
        ),
        out_specs=P("cam", "frame", None, None),
        check_vma=False,
    )
```

```python
import functools
import math

import jax
import jax.numpy as jnp
from jax import lax
from jax.experimental import pallas as pl
from jax.experimental.pallas import tpu as pltpu
from jax.sharding import PartitionSpec as P

HEADS = 8
HEAD = 72
INNER = HEADS * HEAD
EPS = 1e-06
ROW_TOKENS = 64
BIG = 1e30
COEF = HEAD ** (-0.5) * math.log2(math.e)
LANES = 128
KEY_LANES = 640
MIB = 1 << 20


def to_owners(x):
    return lax.all_to_all(x, "frame", split_axis=0, concat_axis=0, tiled=True)


def cam_is_odd():
    return lax.rem(lax.axis_index("cam"), 2)


def exchange_pairs(peers):
    inside, early, late = [], [], []
    for i in range(0, peers, 2):
        inside += [(i, i + 1), (i + 1, i)]
        last = (i + peers - 1) % peers
        (late if (i // 2) % 2 else early).extend([(last, i), (i, last)])
    return inside, early, late


def is_early():
    peers = lax.axis_size("cam")
    return lax.rem(lax.rem(lax.axis_index("cam") + 1, peers) // 2, 2) == 0


def dot_nt(a, b):
    return lax.dot_general(a, b, (((1,), (1,)), ((), ())), preferred_element_type=jnp.float32)


def dot_nn(a, b):
    return lax.dot_general(a, b, (((1,), (0,)), ((), ())), preferred_element_type=jnp.float32)


def normalize(values):
    values = values.astype(jnp.float32)
    mean = jnp.mean(values, axis=-1, keepdims=True)
    centred = values - mean
    variance = jnp.mean(centred * centred, axis=-1, keepdims=True)
    return (centred * lax.rsqrt(variance + EPS)).astype(jnp.bfloat16)


def keys_bias(rows, count):
    position = lax.broadcasted_iota(jnp.int32, (rows, LANES), 0).astype(jnp.float32)
    return jnp.where(position < ROW_TOKENS * count, 0.0, -BIG).astype(jnp.bfloat16)


def key_window(keys, head, bias):
    window = keys[:, head * HEAD : head * HEAD + LANES]
    lane = lax.broadcasted_iota(jnp.int32, window.shape, 1)
    window = jnp.where(lane < HEAD, window, jnp.zeros_like(window))
    return window if bias is None else jnp.where(lane == HEAD, bias, window)


def one_then_zeros(rows, columns):
    return jnp.where(lax.broadcasted_iota(jnp.int32, (rows, columns), 0) == 0, 1.0, 0.0)


def head_rows(x, head):
    return x[head * HEAD : (head + 1) * HEAD, :]


def rounded(x):
    return x.astype(jnp.bfloat16).astype(jnp.float32)


def padded_keys(keys):
    fill = jnp.zeros((keys.shape[0], KEY_LANES - keys.shape[1]), jnp.float32)
    return jnp.concatenate([keys, fill], axis=1).astype(jnp.bfloat16)


def with_side(keys, side):
    return (keys.astype(jnp.float32) + side).astype(jnp.bfloat16)


def side_row(side, neighbours_ref, cam, lower, cameras, cam_here):
    camera = lax.axis_index("cam") * cam_here + cam
    first_lower = neighbours_ref[cam, 0] == lax.rem(camera + cameras - 1, cameras)
    return jnp.where(first_lower == lower, side[0:1, :], side[1:2, :])


def staggered(items, score, rest, ahead):
    scores = [score(item) for item in items[:ahead]]
    for i, item in enumerate(items):
        if i + ahead < len(items):
            scores.append(score(items[i + ahead]))
        rest(item, scores[i])
        scores[i] = None


def camera_rows(cam, rows):
    return pl.ds(pl.multiple_of(cam * rows, rows), rows)


def norm_kernel(counts_ref, tokens_ref, outer_ref, inner_ref):
    rows = tokens_ref.shape[0] // 2
    odd = cam_is_odd()
    for cam, out_ref in ((odd, outer_ref), (1 - odd, inner_ref)):
        out_ref[:rows, :] = normalize(tokens_ref[camera_rows(cam, rows), :])
        count = counts_ref[0, cam].astype(jnp.float32)
        out_ref[rows:, :] = jnp.full((out_ref.shape[0] - rows, out_ref.shape[1]), count, jnp.float32).astype(jnp.bfloat16)


def write_finished(i, pieces, tokens, out_weight_ref, info_ref, mixed_ref, payload_ref):
    attended = jnp.concatenate(pieces, axis=0).T.astype(jnp.bfloat16)
    mixed = (dot_nn(attended, out_weight_ref[...]) + tokens.astype(jnp.float32)).astype(jnp.bfloat16)
    rows, width = mixed.shape
    mixed_ref[...] = mixed
    payload_ref[:rows, :width] = normalize(mixed)
    position = lax.broadcasted_iota(jnp.int32, (rows, LANES), 0).astype(jnp.float32)
    valid = position < ROW_TOKENS * info_ref[2 + i : 3 + i, :LANES]
    payload_ref[:rows, width:] = jnp.where(valid, 1.0, 0.0).astype(jnp.bfloat16)


def local_kernel(
    cameras, counts_ref, neighbours_ref, outer_ref, inner_ref, far_ref, weight_ref, side_ref, tokens_ref, out_weight_ref,
    query_ref, part_ref, info_ref, mixed_ref, payload_ref, value_ref,
):
    rows = mixed_ref.shape[0]
    odd = cam_is_odd()
    cams = (odd, 1 - odd)
    normed = jnp.concatenate([outer_ref[:rows, :], inner_ref[:rows, :], far_ref[:rows, :]], axis=0)
    keys = padded_keys(dot_nt(normed, weight_ref[INNER : 2 * INNER, :]))
    query_ref[...] = rounded(dot_nt(weight_ref[:INNER, :], normed[: 2 * rows]))
    value_ref[...] = rounded(dot_nt(weight_ref[2 * INNER :, :], normed))
    sides = jnp.concatenate(
        [side_ref[...].astype(jnp.float32), jnp.zeros((2, KEY_LANES - INNER), jnp.float32)], axis=1
    )
    far_sides = [side_row(sides, neighbours_ref, cam, cam == 0, cameras, 2) for cam in cams]
    near_sides = [side_row(sides, neighbours_ref, cam, cam == 1, cameras, 2) for cam in cams]
    counts = [counts_ref[0, cam].astype(jnp.float32) for cam in cams]
    info_ref[0:1, :] = far_sides[0]
    info_ref[1:2, :] = far_sides[1]
    for i in range(2):
        info_ref[2 + i : 3 + i, :] = jnp.full((1, KEY_LANES), counts[i], jnp.float32)
    info_ref[4:, :] = jnp.zeros((info_ref.shape[0] - 4, KEY_LANES), jnp.float32)
    biases = [keys_bias(rows, count) for count in counts]
    far_bias = keys_bias(rows, far_ref[rows : rows + 16, :LANES].astype(jnp.float32)[:1])
    one_rows = one_then_zeros(LANES - HEAD, rows)
    value_ones = one_then_zeros(8, 3 * rows)
    outer, inner, far = (slice(i * rows, (i + 1) * rows) for i in range(3))
    kept = (
        (
            outer,
            (outer, inner),
            jnp.concatenate([keys[outer], with_side(keys[inner], near_sides[0])], axis=0),
            jnp.concatenate([biases[0], biases[1]], axis=0),
        ),
        (
            inner,
            (inner, outer, far),
            jnp.concatenate(
                [keys[inner], with_side(keys[outer], near_sides[1]), with_side(keys[far], far_sides[1])], axis=0
            ),
            jnp.concatenate([biases[1], biases[0], far_bias], axis=0),
        ),
    )
    pieces = []

    def score(item):
        i, h = item
        own, _, k_all, bias = kept[i]
        q = jnp.concatenate([head_rows(query_ref[:, own], h), one_rows], axis=0).astype(jnp.bfloat16)
        return dot_nn(key_window(k_all, h, bias), q)

    def rest(item, scores):
        i, h = item
        blocks = kept[i][1]
        highest = jnp.max(scores, axis=0, keepdims=True)
        expo = jnp.exp2((scores - highest) * COEF).astype(jnp.bfloat16)
        v = jnp.concatenate([head_rows(value_ref[:, block], h) for block in blocks], axis=1)
        v = jnp.concatenate([v, value_ones[:, : v.shape[1]]], axis=0).astype(jnp.bfloat16)
        summed = dot_nn(v, expo)
        if i == 0:
            row = lax.broadcasted_iota(jnp.int32, summed.shape, 0)
            part_ref[h] = jnp.where(row == HEAD + 1, highest, summed)
        else:
            pieces.append(summed[:HEAD] * (1.0 / summed[HEAD : HEAD + 1]))

    staggered([(i, h) for i in (1, 0) for h in range(HEADS)], score, rest, 3)
    tokens = tokens_ref[camera_rows(1 - odd, rows), :]
    write_finished(1, pieces, tokens, out_weight_ref, info_ref, mixed_ref, payload_ref)


def outer_kernel(
    early_ref, late_ref, weight_ref, info_ref, query_ref, part_ref, tokens_ref, out_weight_ref, inner_ref, mixed_ref,
    payload_ref, value_ref,
):
    rows = mixed_ref.shape[0]
    early = is_early()
    far = jnp.where(early, early_ref[:rows, :], late_ref[:rows, :])
    far_count = jnp.where(early, early_ref[rows : rows + 16, :LANES], late_ref[rows : rows + 16, :LANES])
    keys = padded_keys(dot_nt(far, weight_ref[INNER : 2 * INNER, :]))
    keys = with_side(keys, info_ref[0:1, :])
    value_ref[...] = rounded(dot_nt(weight_ref[2 * INNER :, :], far))
    payload_ref[rows:, :] = inner_ref[...]
    bias = keys_bias(rows, far_count.astype(jnp.float32)[:1])
    one_rows = one_then_zeros(LANES - HEAD, rows)
    value_ones = one_then_zeros(8, rows)
    pieces = []

    def score(h):
        q = jnp.concatenate([head_rows(query_ref[:, :rows], h), one_rows], axis=0).astype(jnp.bfloat16)
        return dot_nn(key_window(keys, h, bias), q)

    def rest(h, scores):
        part = part_ref[h]
        before = part[HEAD + 1 : HEAD + 2, :]
        highest = jnp.maximum(jnp.max(scores, axis=0, keepdims=True), before)
        expo = jnp.exp2((scores - highest) * COEF).astype(jnp.bfloat16)
        v = jnp.concatenate([head_rows(value_ref[...], h), value_ones], axis=0).astype(jnp.bfloat16)
        summed = part * jnp.exp2((before - highest) * COEF) + dot_nn(v, expo)
        pieces.append(summed[:HEAD] * (1.0 / summed[HEAD : HEAD + 1]))

    staggered(list(range(HEADS)), score, rest, 3)
    tokens = tokens_ref[camera_rows(cam_is_odd(), rows), :]
    write_finished(0, pieces, tokens, out_weight_ref, info_ref, mixed_ref, payload_ref)


def swap_halves(first, second):
    upper = lax.broadcasted_iota(jnp.int32, first.shape, 1) < 4
    return jnp.where(upper, first, pltpu.roll(second, 4, 1)), jnp.where(upper, pltpu.roll(first, 4, 1), second)


def time_kernel(frames, payload_ref, weight_ref, out_ref, query_ref, value_ref):
    rows, lanes = payload_ref.shape
    model = weight_ref.shape[1]
    half = rows // 2
    places = half // frames
    pairs = payload_ref[...].astype(jnp.float32).reshape(frames // 2, 2, 2 * places, lanes)
    low, high = swap_halves(pairs[:, 0], pairs[:, 1])
    payload = jnp.concatenate([low.reshape(half, lanes), high.reshape(half, lanes)], axis=0).astype(jnp.bfloat16)
    normed = payload[:, :model]
    keys = padded_keys(dot_nt(normed, weight_ref[INNER : 2 * INNER, :]))
    query_ref[...] = rounded(dot_nt(weight_ref[:INNER, :], normed))
    value_ref[...] = rounded(dot_nt(weight_ref[2 * INNER :, :], normed))
    lane = lax.broadcasted_iota(jnp.int32, (rows, LANES), 1)
    key = lax.rem(lax.broadcasted_iota(jnp.int32, (rows, LANES), 0), half)
    invalid = payload[:, model:].astype(jnp.float32) < 0.5
    key_mask = jnp.where(
        lane < frames,
        jnp.where(jnp.logical_and(invalid, lane != key // places), -BIG, 0.0),
        jnp.where(lane - frames == key % places, 1.0, 0.0),
    ).astype(jnp.bfloat16)
    entry = lax.broadcasted_iota(jnp.int32, (LANES, half), 0)
    query = lax.broadcasted_iota(jnp.int32, (LANES, half), 1)
    query_mask = jnp.where(
        entry < frames,
        jnp.where(entry == query // places, 1.0, 0.0),
        jnp.where(jnp.logical_and(entry < frames + places, entry - frames != query % places), -BIG, 0.0),
    ).astype(jnp.bfloat16)
    zero_rows = jnp.zeros((LANES - HEAD, half), jnp.float32)
    value_ones = one_then_zeros(8, half)
    pieces = [[], []]

    def score(item):
        h, b = item
        here = slice(b * half, (b + 1) * half)
        q = jnp.concatenate([head_rows(query_ref[:, here], h), zero_rows], axis=0).astype(jnp.bfloat16)
        return dot_nn(
            jnp.concatenate([key_window(keys[here], h, None), key_mask[here]], axis=1),
            jnp.concatenate([q, query_mask], axis=0),
        )

    def rest(item, scores):
        h, b = item
        highest = jnp.max(scores, axis=0, keepdims=True)
        expo = jnp.exp2((scores - highest) * COEF).astype(jnp.bfloat16)
        v = head_rows(value_ref[:, b * half : (b + 1) * half], h)
        summed = dot_nn(jnp.concatenate([v, value_ones], axis=0).astype(jnp.bfloat16), expo)
        pieces[b].append(summed[:HEAD] * (1.0 / summed[HEAD : HEAD + 1]))

    staggered([(h, b) for h in range(HEADS) for b in range(2)], score, rest, 4)
    blocks = [jnp.concatenate(piece, axis=0).T.reshape(frames // 2, 2 * places, INNER) for piece in pieces]
    out_ref[...] = jnp.stack(swap_halves(*blocks), axis=1).reshape(rows, INNER).astype(jnp.bfloat16)


def final_kernel(attended_ref, weight_ref, outer_ref, inner_ref, out_hbm, block_ref, sems):
    rows = outer_ref.shape[0]
    size = block_ref.shape[1]
    odd = cam_is_odd()
    copies = []
    for i, (cam, mixed_ref) in enumerate(((odd, outer_ref), (1 - odd, inner_ref))):
        for start in range(0, rows, size):
            slot = len(copies)
            result = dot_nn(attended_ref[i * rows + start : i * rows + start + size, :], weight_ref[...])
            result = result + mixed_ref[start : start + size, :].astype(jnp.float32)
            block_ref[slot] = result.astype(jnp.bfloat16)
            there = pl.ds(pl.multiple_of(cam * rows + start, size), size)
            copies.append(pltpu.make_async_copy(block_ref.at[slot], out_hbm.at[there], sems.at[slot]))
            copies[-1].start()
    for copy in copies:
        copy.wait()


SMEM = pl.BlockSpec(memory_space=pltpu.SMEM)
VMEM = pl.BlockSpec(memory_space=pltpu.VMEM)
ANY = pl.BlockSpec(memory_space=pl.ANY)


def kernel_call(body, ins, outs, scratch, mib, flops, nbytes, out_space=VMEM):
    return pl.pallas_call(
        body,
        out_shape=outs,
        in_specs=ins,
        out_specs=[out_space] * len(outs),
        scratch_shapes=scratch,
        compiler_params=pltpu.CompilerParams(vmem_limit_bytes=mib * MIB),
        cost_estimate=pl.CostEstimate(flops=flops, bytes_accessed=nbytes, transcendentals=0),
    )


def shards(tokens, counts, neighbours, side_keys, cross_qkv, cross_out, time_qkv, time_out):
    cam_here, frames_here, token_count, model = tokens.shape
    cameras = cam_here * lax.axis_size("cam")
    frames = lax.axis_size("frame")
    rows = cam_here * token_count
    bf16 = jnp.bfloat16
    spread = functools.partial(jax.ShapeDtypeStruct, dtype=bf16)

    flat = tokens.reshape(rows, model)
    own_counts = counts.reshape(1, cam_here)
    cross_t, time_t = cross_qkv.T, time_qkv.T
    inside_pairs, early_pairs, late_pairs = exchange_pairs(lax.axis_size("cam"))
    sent = token_count + 16

    outer, inner = kernel_call(
        norm_kernel, [SMEM, VMEM], [spread((sent, model))] * 2, [], 16, 6_000_000_000, 2_400_000
    )(own_counts, flat)
    early_far = lax.ppermute(outer, "cam", early_pairs)
    inner_far = lax.ppermute(inner, "cam", inside_pairs)

    query, part, info, mixed_inner, payload_inner = kernel_call(
        functools.partial(local_kernel, cameras),
        [SMEM, SMEM] + [VMEM] * 7,
        [
            jax.ShapeDtypeStruct((INNER, rows), jnp.float32),
            jax.ShapeDtypeStruct((HEADS, HEAD + 8, token_count), jnp.float32),
            jax.ShapeDtypeStruct((8, KEY_LANES), jnp.float32),
            spread((token_count, model)),
            spread((token_count, model + LANES)),
        ],
        [pltpu.VMEM((INNER, rows + token_count), jnp.float32)],
        36,
        8_000_000_000,
        20_000_000,
    )(own_counts, neighbours, outer, inner, inner_far, cross_t, side_keys, flat, cross_out)
    outer, payload_inner = lax.optimization_barrier((outer, payload_inner))
    late_far = lax.ppermute(outer, "cam", late_pairs)
    mixed_outer, payload = kernel_call(
        outer_kernel,
        [VMEM] * 9,
        [spread((token_count, model)), spread((rows, model + LANES))],
        [pltpu.VMEM((INNER, token_count), jnp.float32)],
        32,
        2_500_000_000,
        8_000_000,
    )(early_far, late_far, cross_t, info, query, part, flat, cross_out, payload_inner)

    chunk = rows // frames
    arrived = to_owners(payload.reshape(frames, chunk, model + LANES))
    (attended,) = kernel_call(
        functools.partial(time_kernel, frames),
        [VMEM] * 2,
        [spread((rows, INNER))],
        [pltpu.VMEM((INNER, rows), jnp.float32)] * 2,
        32,
        6_000_000_000,
        10_000_000,
    )(arrived.reshape(rows, model + LANES), time_t)
    returned = to_owners(attended.reshape(frames, chunk, INNER))
    (out,) = kernel_call(
        final_kernel,
        [VMEM] * 4,
        [spread((rows, model))],
        [pltpu.VMEM((4, rows // 4, model), bf16), pltpu.SemaphoreType.DMA((4,))],
        32,
        700_000_000,
        4_000_000,
        ANY,
    )(returned.reshape(rows, INNER), time_out, mixed_outer, mixed_inner)
    return out.reshape(tokens.shape)


def solution(mesh):
    return jax.shard_map(
        shards,
        mesh=mesh,
        in_specs=(
            P("cam", "frame", None, None),
            P("cam", "frame"),
            P("cam", None),
            P(),
            P(),
            P(),
            P(),
            P(),
        ),
        out_specs=P("cam", "frame", None, None),
        check_vma=False,
    )
```

```python
import functools
import math

import jax
import jax.numpy as jnp
from jax import lax
from jax.experimental import pallas as pl
from jax.experimental.pallas import tpu as pltpu
from jax.sharding import PartitionSpec as P

HEADS = 8
HEAD = 72
INNER = HEADS * HEAD
EPS = 1e-06
ROW_TOKENS = 64
BIG = 1e30
COEF = HEAD ** (-0.5) * math.log2(math.e)
LANES = 128
KEY_LANES = 640
PLACES = 2
GROUPS = 4
MIB = 1 << 20


def to_owners(x):
    return lax.all_to_all(x, "frame", split_axis=0, concat_axis=0, tiled=True)


def cam_is_odd():
    return lax.rem(lax.axis_index("cam"), 2)


def exchange_pairs(peers):
    inside, early, late = [], [], []
    for i in range(0, peers, 2):
        inside += [(i, i + 1), (i + 1, i)]
        last = (i + peers - 1) % peers
        (late if (i // 2) % 2 else early).extend([(last, i), (i, last)])
    return inside, early, late


def is_early():
    peers = lax.axis_size("cam")
    return lax.rem(lax.rem(lax.axis_index("cam") + 1, peers) // 2, 2) == 0


def dot_nt(a, b):
    return lax.dot_general(a, b, (((1,), (1,)), ((), ())), preferred_element_type=jnp.float32)


def dot_nn(a, b):
    return lax.dot_general(a, b, (((1,), (0,)), ((), ())), preferred_element_type=jnp.float32)


def normalize(values):
    values = values.astype(jnp.float32)
    mean = jnp.mean(values, axis=-1, keepdims=True)
    centred = values - mean
    variance = jnp.mean(centred * centred, axis=-1, keepdims=True)
    return (centred * lax.rsqrt(variance + EPS)).astype(jnp.bfloat16)


def keys_bias(rows, count):
    position = lax.broadcasted_iota(jnp.int32, (rows, LANES), 0).astype(jnp.float32)
    return jnp.where(position < ROW_TOKENS * count, 0.0, -BIG).astype(jnp.bfloat16)


def key_window(keys, head, bias):
    window = keys[:, head * HEAD : head * HEAD + LANES]
    lane = lax.broadcasted_iota(jnp.int32, window.shape, 1)
    window = jnp.where(lane < HEAD, window, jnp.zeros_like(window))
    return window if bias is None else jnp.where(lane == HEAD, bias, window)


def one_then_zeros(rows, columns):
    return jnp.where(lax.broadcasted_iota(jnp.int32, (rows, columns), 0) == 0, 1.0, 0.0)


def head_rows(x, head):
    return x[head * HEAD : (head + 1) * HEAD, :]


def rounded(x):
    return x.astype(jnp.bfloat16).astype(jnp.float32)


def padded_keys(keys):
    fill = jnp.zeros((keys.shape[0], KEY_LANES - keys.shape[1]), jnp.float32)
    return jnp.concatenate([keys, fill], axis=1).astype(jnp.bfloat16)


def with_side(keys, side):
    return (keys.astype(jnp.float32) + side).astype(jnp.bfloat16)


def side_row(side, neighbours_ref, cam, lower, cameras, cam_here):
    camera = lax.axis_index("cam") * cam_here + cam
    first_lower = neighbours_ref[cam, 0] == lax.rem(camera + cameras - 1, cameras)
    return jnp.where(first_lower == lower, side[0:1, :], side[1:2, :])


def staggered(items, score, rest, ahead):
    scores = [score(item) for item in items[:ahead]]
    for i, item in enumerate(items):
        if i + ahead < len(items):
            scores.append(score(items[i + ahead]))
        rest(item, scores[i])
        scores[i] = None


def camera_rows(cam, rows):
    return pl.ds(pl.multiple_of(cam * rows, rows), rows)


def norm_kernel(counts_ref, tokens_ref, outer_ref, inner_ref):
    rows = tokens_ref.shape[0] // 2
    odd = cam_is_odd()
    for cam, out_ref in ((odd, outer_ref), (1 - odd, inner_ref)):
        out_ref[:rows, :] = normalize(tokens_ref[camera_rows(cam, rows), :])
        count = counts_ref[0, cam].astype(jnp.float32)
        out_ref[rows:, :] = jnp.full((out_ref.shape[0] - rows, out_ref.shape[1]), count, jnp.float32).astype(jnp.bfloat16)


def write_finished(i, pieces, tokens, out_weight_ref, info_ref, mixed_ref, payload_ref):
    attended = jnp.concatenate(pieces, axis=0).T.astype(jnp.bfloat16)
    mixed = (dot_nn(attended, out_weight_ref[...]) + tokens.astype(jnp.float32)).astype(jnp.bfloat16)
    rows, width = mixed.shape
    mixed_ref[...] = mixed
    normed = normalize(mixed)
    size = rows // GROUPS
    chunks = size // PLACES
    for g in range(GROUPS):
        block = normed[g * size : (g + 1) * size].reshape(chunks, PLACES, width)
        payload_ref[:chunks, :, g * width : (g + 1) * width] = block
    group = lax.broadcasted_iota(jnp.int32, (size, LANES), 1) // (LANES // GROUPS)
    position = lax.broadcasted_iota(jnp.int32, (size, LANES), 0) + group * size
    valid = position.astype(jnp.float32) < ROW_TOKENS * info_ref[2 + i : 3 + i, :LANES]
    valid = jnp.where(valid, 1.0, 0.0).astype(jnp.bfloat16)
    payload_ref[:chunks, :, GROUPS * width :] = valid.reshape(chunks, PLACES, LANES)


def local_kernel(
    cameras, counts_ref, neighbours_ref, outer_ref, inner_ref, far_ref, weight_ref, side_ref, tokens_ref, out_weight_ref,
    query_ref, part_ref, info_ref, mixed_ref, payload_ref, value_ref,
):
    rows = mixed_ref.shape[0]
    odd = cam_is_odd()
    cams = (odd, 1 - odd)
    normed = jnp.concatenate([outer_ref[:rows, :], inner_ref[:rows, :], far_ref[:rows, :]], axis=0)
    keys = padded_keys(dot_nt(normed, weight_ref[INNER : 2 * INNER, :]))
    query_ref[...] = rounded(dot_nt(weight_ref[:INNER, :], normed[: 2 * rows]))
    value_ref[...] = rounded(dot_nt(weight_ref[2 * INNER :, :], normed))
    sides = jnp.concatenate(
        [side_ref[...].astype(jnp.float32), jnp.zeros((2, KEY_LANES - INNER), jnp.float32)], axis=1
    )
    far_sides = [side_row(sides, neighbours_ref, cam, cam == 0, cameras, 2) for cam in cams]
    near_sides = [side_row(sides, neighbours_ref, cam, cam == 1, cameras, 2) for cam in cams]
    counts = [counts_ref[0, cam].astype(jnp.float32) for cam in cams]
    info_ref[0:1, :] = far_sides[0]
    info_ref[1:2, :] = far_sides[1]
    for i in range(2):
        info_ref[2 + i : 3 + i, :] = jnp.full((1, KEY_LANES), counts[i], jnp.float32)
    info_ref[4:, :] = jnp.zeros((info_ref.shape[0] - 4, KEY_LANES), jnp.float32)
    biases = [keys_bias(rows, count) for count in counts]
    far_bias = keys_bias(rows, far_ref[rows : rows + 16, :LANES].astype(jnp.float32)[:1])
    one_rows = one_then_zeros(LANES - HEAD, rows)
    value_ones = one_then_zeros(8, 3 * rows)
    outer, inner, far = (slice(i * rows, (i + 1) * rows) for i in range(3))
    kept = (
        (
            outer,
            (outer, inner),
            jnp.concatenate([keys[outer], with_side(keys[inner], near_sides[0])], axis=0),
            jnp.concatenate([biases[0], biases[1]], axis=0),
        ),
        (
            inner,
            (inner, outer, far),
            jnp.concatenate(
                [keys[inner], with_side(keys[outer], near_sides[1]), with_side(keys[far], far_sides[1])], axis=0
            ),
            jnp.concatenate([biases[1], biases[0], far_bias], axis=0),
        ),
    )
    pieces = []

    def score(item):
        i, h = item
        own, _, k_all, bias = kept[i]
        q = jnp.concatenate([head_rows(query_ref[:, own], h), one_rows], axis=0).astype(jnp.bfloat16)
        return dot_nn(key_window(k_all, h, bias), q)

    def rest(item, scores):
        i, h = item
        blocks = kept[i][1]
        highest = jnp.max(scores, axis=0, keepdims=True)
        expo = jnp.exp2((scores - highest) * COEF).astype(jnp.bfloat16)
        v = jnp.concatenate([head_rows(value_ref[:, block], h) for block in blocks], axis=1)
        v = jnp.concatenate([v, value_ones[:, : v.shape[1]]], axis=0).astype(jnp.bfloat16)
        summed = dot_nn(v, expo)
        if i == 0:
            row = lax.broadcasted_iota(jnp.int32, summed.shape, 0)
            part_ref[h] = jnp.where(row == HEAD + 1, highest, summed)
        else:
            pieces.append(summed[:HEAD] * (1.0 / summed[HEAD : HEAD + 1]))

    staggered([(i, h) for i in (1, 0) for h in range(HEADS)], score, rest, 3)
    tokens = tokens_ref[camera_rows(1 - odd, rows), :]
    write_finished(1, pieces, tokens, out_weight_ref, info_ref, mixed_ref, payload_ref)


def outer_kernel(
    early_ref, late_ref, weight_ref, info_ref, query_ref, part_ref, tokens_ref, out_weight_ref, inner_ref, mixed_ref,
    payload_ref, value_ref,
):
    rows = mixed_ref.shape[0]
    early = is_early()
    far = jnp.where(early, early_ref[:rows, :], late_ref[:rows, :])
    far_count = jnp.where(early, early_ref[rows : rows + 16, :LANES], late_ref[rows : rows + 16, :LANES])
    keys = padded_keys(dot_nt(far, weight_ref[INNER : 2 * INNER, :]))
    keys = with_side(keys, info_ref[0:1, :])
    value_ref[...] = rounded(dot_nt(weight_ref[2 * INNER :, :], far))
    payload_ref[inner_ref.shape[0] :] = inner_ref[...]
    bias = keys_bias(rows, far_count.astype(jnp.float32)[:1])
    one_rows = one_then_zeros(LANES - HEAD, rows)
    value_ones = one_then_zeros(8, rows)
    pieces = []

    def score(h):
        q = jnp.concatenate([head_rows(query_ref[:, :rows], h), one_rows], axis=0).astype(jnp.bfloat16)
        return dot_nn(key_window(keys, h, bias), q)

    def rest(h, scores):
        part = part_ref[h]
        before = part[HEAD + 1 : HEAD + 2, :]
        highest = jnp.maximum(jnp.max(scores, axis=0, keepdims=True), before)
        expo = jnp.exp2((scores - highest) * COEF).astype(jnp.bfloat16)
        v = jnp.concatenate([head_rows(value_ref[...], h), value_ones], axis=0).astype(jnp.bfloat16)
        summed = part * jnp.exp2((before - highest) * COEF) + dot_nn(v, expo)
        pieces.append(summed[:HEAD] * (1.0 / summed[HEAD : HEAD + 1]))

    staggered(list(range(HEADS)), score, rest, HEADS)
    tokens = tokens_ref[camera_rows(cam_is_odd(), rows), :]
    write_finished(0, pieces, tokens, out_weight_ref, info_ref, mixed_ref, payload_ref)


def time_kernel(frames, payload_ref, weight_ref, out_ref, query_ref, value_ref):
    size = frames * PLACES
    rows = GROUPS * size
    model = weight_ref.shape[1]
    normed = jnp.concatenate(
        [payload_ref[:, :, g * model : (g + 1) * model].reshape(size, model) for g in range(GROUPS)], axis=0
    )
    keys = padded_keys(dot_nt(normed, weight_ref[INNER : 2 * INNER, :]))
    query_ref[...] = rounded(dot_nt(weight_ref[:INNER, :], normed))
    value_ref[...] = rounded(dot_nt(weight_ref[2 * INNER :, :], normed))
    valid = payload_ref[:, :, GROUPS * model :].reshape(size, LANES).astype(jnp.float32)
    lane = lax.broadcasted_iota(jnp.int32, (size, LANES), 1)
    key = lax.broadcasted_iota(jnp.int32, (size, LANES), 0)
    key_masks = []
    for g in range(GROUPS):
        first = g * (LANES // GROUPS)
        invalid = valid[:, first : first + 1] < 0.5
        key_mask = jnp.where(
            lane < frames,
            jnp.where(jnp.logical_and(invalid, lane != key // PLACES), -BIG, 0.0),
            jnp.where(lane - frames == key % PLACES, 1.0, 0.0),
        )
        key_masks.append(key_mask.astype(jnp.bfloat16))
    entry = lax.broadcasted_iota(jnp.int32, (LANES, size), 0)
    query = lax.broadcasted_iota(jnp.int32, (LANES, size), 1)
    query_mask = jnp.where(
        entry < frames,
        jnp.where(entry == query // PLACES, 1.0, 0.0),
        jnp.where(jnp.logical_and(entry < frames + PLACES, entry - frames != query % PLACES), -BIG, 0.0),
    ).astype(jnp.bfloat16)
    zero_rows = jnp.zeros((LANES - HEAD, size), jnp.float32)
    value_ones = one_then_zeros(8, size)
    pieces = [[] for _ in range(GROUPS)]

    def score(item):
        h, g = item
        here = slice(g * size, (g + 1) * size)
        q = jnp.concatenate([head_rows(query_ref[:, here], h), zero_rows], axis=0).astype(jnp.bfloat16)
        return dot_nn(
            jnp.concatenate([key_window(keys[here], h, None), key_masks[g]], axis=1),
            jnp.concatenate([q, query_mask], axis=0),
        )

    def rest(item, scores):
        h, g = item
        highest = jnp.max(scores, axis=0, keepdims=True)
        expo = jnp.exp2((scores - highest) * COEF).astype(jnp.bfloat16)
        v = head_rows(value_ref[:, g * size : (g + 1) * size], h)
        summed = dot_nn(jnp.concatenate([v, value_ones], axis=0).astype(jnp.bfloat16), expo)
        pieces[g].append(summed[:HEAD] * (1.0 / summed[HEAD : HEAD + 1]))

    staggered([(h, g) for h in range(HEADS) for g in range(GROUPS)], score, rest, 6)
    attended = jnp.concatenate(sum(pieces, []), axis=0).T.astype(jnp.bfloat16)
    out_ref[...] = attended.reshape(frames, PLACES, GROUPS * INNER)


def final_kernel(attended_ref, weight_ref, outer_ref, inner_ref, out_hbm, block_ref, sems):
    rows = outer_ref.shape[0]
    size = rows // GROUPS
    chunks = size // PLACES
    half = GROUPS // 2
    odd = cam_is_odd()
    copies = []
    for i, (cam, mixed_ref) in enumerate(((odd, outer_ref), (1 - odd, inner_ref))):
        here = slice(i * chunks, (i + 1) * chunks)
        blocks = [
            attended_ref[here, :, g * INNER : (g + 1) * INNER].reshape(size, INNER) for g in range(GROUPS)
        ]
        for part in range(2):
            slot = len(copies)
            start = part * half * size
            attended = jnp.concatenate(blocks[part * half : (part + 1) * half], axis=0)
            result = dot_nn(attended, weight_ref[...])
            result = result + mixed_ref[start : start + half * size, :].astype(jnp.float32)
            block_ref[slot] = result.astype(jnp.bfloat16)
            there = pl.ds(pl.multiple_of(cam * rows + start, half * size), half * size)
            copies.append(pltpu.make_async_copy(block_ref.at[slot], out_hbm.at[there], sems.at[slot]))
            copies[-1].start()
    for copy in copies:
        copy.wait()


SMEM = pl.BlockSpec(memory_space=pltpu.SMEM)
VMEM = pl.BlockSpec(memory_space=pltpu.VMEM)
ANY = pl.BlockSpec(memory_space=pl.ANY)


def kernel_call(body, ins, outs, scratch, mib, flops, nbytes, out_space=VMEM):
    return pl.pallas_call(
        body,
        out_shape=outs,
        in_specs=ins,
        out_specs=[out_space] * len(outs),
        scratch_shapes=scratch,
        compiler_params=pltpu.CompilerParams(vmem_limit_bytes=mib * MIB),
        cost_estimate=pl.CostEstimate(flops=flops, bytes_accessed=nbytes, transcendentals=0),
    )


def shards(tokens, counts, neighbours, side_keys, cross_qkv, cross_out, time_qkv, time_out):
    cam_here, frames_here, token_count, model = tokens.shape
    cameras = cam_here * lax.axis_size("cam")
    frames = lax.axis_size("frame")
    rows = cam_here * token_count
    bf16 = jnp.bfloat16
    spread = functools.partial(jax.ShapeDtypeStruct, dtype=bf16)

    flat = tokens.reshape(rows, model)
    payload_lanes = GROUPS * model + LANES
    own_counts = counts.reshape(1, cam_here)
    cross_t, time_t = cross_qkv.T, time_qkv.T
    inside_pairs, early_pairs, late_pairs = exchange_pairs(lax.axis_size("cam"))
    sent = token_count + 16

    outer, inner = kernel_call(
        norm_kernel, [SMEM, VMEM], [spread((sent, model))] * 2, [], 16, 6_000_000_000, 2_400_000
    )(own_counts, flat)
    early_far = lax.ppermute(outer, "cam", early_pairs)
    inner_far = lax.ppermute(inner, "cam", inside_pairs)

    query, part, info, mixed_inner, payload_inner = kernel_call(
        functools.partial(local_kernel, cameras),
        [SMEM, SMEM] + [VMEM] * 7,
        [
            jax.ShapeDtypeStruct((INNER, rows), jnp.float32),
            jax.ShapeDtypeStruct((HEADS, HEAD + 8, token_count), jnp.float32),
            jax.ShapeDtypeStruct((8, KEY_LANES), jnp.float32),
            spread((token_count, model)),
            spread((frames // 2, PLACES, payload_lanes)),
        ],
        [pltpu.VMEM((INNER, rows + token_count), jnp.float32)],
        36,
        8_000_000_000,
        20_000_000,
    )(own_counts, neighbours, outer, inner, inner_far, cross_t, side_keys, flat, cross_out)
    outer, payload_inner = lax.optimization_barrier((outer, payload_inner))
    late_far = lax.ppermute(outer, "cam", late_pairs)
    mixed_outer, payload = kernel_call(
        outer_kernel,
        [VMEM] * 9,
        [spread((token_count, model)), spread((frames, PLACES, payload_lanes))],
        [pltpu.VMEM((INNER, token_count), jnp.float32)],
        32,
        2_500_000_000,
        8_000_000,
    )(early_far, late_far, cross_t, info, query, part, flat, cross_out, payload_inner)

    arrived = to_owners(payload)
    (attended,) = kernel_call(
        functools.partial(time_kernel, frames),
        [VMEM] * 2,
        [spread((frames, PLACES, GROUPS * INNER))],
        [pltpu.VMEM((INNER, rows), jnp.float32)] * 2,
        32,
        6_000_000_000,
        10_000_000,
    )(arrived, time_t)
    returned = to_owners(attended)
    (out,) = kernel_call(
        final_kernel,
        [VMEM] * 4,
        [spread((rows, model))],
        [pltpu.VMEM((4, rows // 4, model), bf16), pltpu.SemaphoreType.DMA((4,))],
        32,
        700_000_000,
        4_000_000,
        ANY,
    )(returned, time_out, mixed_outer, mixed_inner)
    return out.reshape(tokens.shape)


def solution(mesh):
    return jax.shard_map(
        shards,
        mesh=mesh,
        in_specs=(
            P("cam", "frame", None, None),
            P("cam", "frame"),
            P("cam", None),
            P(),
            P(),
            P(),
            P(),
            P(),
        ),
        out_specs=P("cam", "frame", None, None),
        check_vma=False,
    )
```

```python
import functools
import math

import jax
import jax.numpy as jnp
from jax import lax
from jax.experimental import pallas as pl
from jax.experimental.pallas import tpu as pltpu
from jax.sharding import PartitionSpec as P

HEADS = 8
HEAD = 72
INNER = HEADS * HEAD
EPS = 1e-06
ROW_TOKENS = 64
BIG = 1e30
COEF = HEAD ** (-0.5) * math.log2(math.e)
LANES = 128
KEY_LANES = 640
PLACES = 2
GROUPS = 4
MIB = 1 << 20


def to_owners(x):
    return lax.all_to_all(x, "frame", split_axis=0, concat_axis=0, tiled=True)


def cam_is_odd():
    return lax.rem(lax.axis_index("cam"), 2)


def exchange_pairs(peers):
    inside, early, late = [], [], []
    for i in range(0, peers, 2):
        inside += [(i, i + 1), (i + 1, i)]
        last = (i + peers - 1) % peers
        (late if (i // 2) % 2 else early).extend([(last, i), (i, last)])
    return inside, early, late


def is_early():
    peers = lax.axis_size("cam")
    return lax.rem(lax.rem(lax.axis_index("cam") + 1, peers) // 2, 2) == 0


def dot_nt(a, b):
    return lax.dot_general(a, b, (((1,), (1,)), ((), ())), preferred_element_type=jnp.float32)


def dot_nn(a, b):
    return lax.dot_general(a, b, (((1,), (0,)), ((), ())), preferred_element_type=jnp.float32)


def normalize(values):
    values = values.astype(jnp.float32)
    mean = jnp.mean(values, axis=-1, keepdims=True)
    centred = values - mean
    variance = jnp.mean(centred * centred, axis=-1, keepdims=True)
    return (centred * lax.rsqrt(variance + EPS)).astype(jnp.bfloat16)


def keys_bias(rows, count):
    position = lax.broadcasted_iota(jnp.int32, (rows, LANES), 0).astype(jnp.float32)
    return jnp.where(position < ROW_TOKENS * count, 0.0, -BIG).astype(jnp.bfloat16)


def key_window(keys, head, bias):
    window = keys[:, head * HEAD : head * HEAD + LANES]
    lane = lax.broadcasted_iota(jnp.int32, window.shape, 1)
    window = jnp.where(lane < HEAD, window, jnp.zeros_like(window))
    return window if bias is None else jnp.where(lane == HEAD, bias, window)


def one_then_zeros(rows, columns):
    return jnp.where(lax.broadcasted_iota(jnp.int32, (rows, columns), 0) == 0, 1.0, 0.0)


def head_rows(x, head):
    return x[head * HEAD : (head + 1) * HEAD, :]


def rounded(x):
    return x.astype(jnp.bfloat16).astype(jnp.float32)


def padded_keys(keys):
    fill = jnp.zeros((keys.shape[0], KEY_LANES - keys.shape[1]), jnp.float32)
    return jnp.concatenate([keys, fill], axis=1).astype(jnp.bfloat16)


def with_side(keys, side):
    return (keys.astype(jnp.float32) + side).astype(jnp.bfloat16)


def side_row(side, neighbours_ref, cam, lower, cameras, cam_here):
    camera = lax.axis_index("cam") * cam_here + cam
    first_lower = neighbours_ref[cam, 0] == lax.rem(camera + cameras - 1, cameras)
    return jnp.where(first_lower == lower, side[0:1, :], side[1:2, :])


def staggered(items, score, rest, ahead):
    scores = [score(item) for item in items[:ahead]]
    for i, item in enumerate(items):
        if i + ahead < len(items):
            scores.append(score(items[i + ahead]))
        rest(item, scores[i])
        scores[i] = None


def camera_rows(cam, rows):
    return pl.ds(pl.multiple_of(cam * rows, rows), rows)


def norm_kernel(counts_ref, tokens_ref, outer_ref, inner_ref):
    rows = tokens_ref.shape[0] // 2
    odd = cam_is_odd()
    for cam, out_ref in ((odd, outer_ref), (1 - odd, inner_ref)):
        last, *block = out_ref.shape
        last -= 1
        out_ref[:last] = normalize(tokens_ref[camera_rows(cam, rows), :]).reshape(last, *block)
        count = counts_ref[0, cam].astype(jnp.float32)
        out_ref[last:] = jnp.full((1, *block), count, jnp.float32).astype(jnp.bfloat16)


def sent_rows(ref):
    blocks, size, width = ref.shape
    return ref[: blocks - 1].reshape((blocks - 1) * size, width)


def sent_count(ref):
    return ref[ref.shape[0] - 1, :, :LANES].astype(jnp.float32)[:1]


def write_finished(i, pieces, tokens, out_weight_ref, info_ref, mixed_ref, payload_ref):
    attended = jnp.concatenate(pieces, axis=0).T.astype(jnp.bfloat16)
    mixed = (dot_nn(attended, out_weight_ref[...]) + tokens.astype(jnp.float32)).astype(jnp.bfloat16)
    rows, width = mixed.shape
    mixed_ref[...] = mixed
    normed = normalize(mixed)
    size = rows // GROUPS
    chunks = size // PLACES
    for g in range(GROUPS):
        block = normed[g * size : (g + 1) * size].reshape(chunks, PLACES, width)
        payload_ref[:chunks, :, g * width : (g + 1) * width] = block
    group = lax.broadcasted_iota(jnp.int32, (size, LANES), 1) // (LANES // GROUPS)
    position = lax.broadcasted_iota(jnp.int32, (size, LANES), 0) + group * size
    valid = position.astype(jnp.float32) < ROW_TOKENS * info_ref[2 + i : 3 + i, :LANES]
    valid = jnp.where(valid, 1.0, 0.0).astype(jnp.bfloat16)
    payload_ref[:chunks, :, GROUPS * width :] = valid.reshape(chunks, PLACES, LANES)


def local_kernel(
    cameras, counts_ref, neighbours_ref, outer_ref, inner_ref, far_ref, weight_ref, side_ref, tokens_ref, out_weight_ref,
    query_ref, part_ref, info_ref, mixed_ref, payload_ref, value_ref,
):
    rows = mixed_ref.shape[0]
    odd = cam_is_odd()
    cams = (odd, 1 - odd)
    normed = jnp.concatenate([sent_rows(ref) for ref in (outer_ref, inner_ref, far_ref)], axis=0)
    keys = padded_keys(dot_nt(normed, weight_ref[INNER : 2 * INNER, :]))
    query_ref[...] = rounded(dot_nt(weight_ref[:INNER, :], normed[: 2 * rows]))
    value_ref[...] = rounded(dot_nt(weight_ref[2 * INNER :, :], normed))
    sides = jnp.concatenate(
        [side_ref[...].astype(jnp.float32), jnp.zeros((2, KEY_LANES - INNER), jnp.float32)], axis=1
    )
    far_sides = [side_row(sides, neighbours_ref, cam, cam == 0, cameras, 2) for cam in cams]
    near_sides = [side_row(sides, neighbours_ref, cam, cam == 1, cameras, 2) for cam in cams]
    counts = [counts_ref[0, cam].astype(jnp.float32) for cam in cams]
    info_ref[0:1, :] = far_sides[0]
    info_ref[1:2, :] = far_sides[1]
    for i in range(2):
        info_ref[2 + i : 3 + i, :] = jnp.full((1, KEY_LANES), counts[i], jnp.float32)
    info_ref[4:, :] = jnp.zeros((info_ref.shape[0] - 4, KEY_LANES), jnp.float32)
    biases = [keys_bias(rows, count) for count in counts]
    far_bias = keys_bias(rows, sent_count(far_ref))
    one_rows = one_then_zeros(LANES - HEAD, rows)
    value_ones = one_then_zeros(8, 3 * rows)
    outer, inner, far = (slice(i * rows, (i + 1) * rows) for i in range(3))
    kept = (
        (
            outer,
            (outer, inner),
            jnp.concatenate([keys[outer], with_side(keys[inner], near_sides[0])], axis=0),
            jnp.concatenate([biases[0], biases[1]], axis=0),
        ),
        (
            inner,
            (inner, outer, far),
            jnp.concatenate(
                [keys[inner], with_side(keys[outer], near_sides[1]), with_side(keys[far], far_sides[1])], axis=0
            ),
            jnp.concatenate([biases[1], biases[0], far_bias], axis=0),
        ),
    )
    pieces = []

    def score(item):
        i, h = item
        own, _, k_all, bias = kept[i]
        q = jnp.concatenate([head_rows(query_ref[:, own], h), one_rows], axis=0).astype(jnp.bfloat16)
        return dot_nn(key_window(k_all, h, bias), q)

    def rest(item, scores):
        i, h = item
        blocks = kept[i][1]
        highest = jnp.max(scores, axis=0, keepdims=True)
        expo = jnp.exp2((scores - highest) * COEF).astype(jnp.bfloat16)
        v = jnp.concatenate([head_rows(value_ref[:, block], h) for block in blocks], axis=1)
        v = jnp.concatenate([v, value_ones[:, : v.shape[1]]], axis=0).astype(jnp.bfloat16)
        summed = dot_nn(v, expo)
        if i == 0:
            row = lax.broadcasted_iota(jnp.int32, summed.shape, 0)
            part_ref[h] = jnp.where(row == HEAD + 1, highest, summed)
        else:
            pieces.append(summed[:HEAD] * (1.0 / summed[HEAD : HEAD + 1]))

    staggered([(i, h) for i in (1, 0) for h in range(HEADS)], score, rest, 8)
    tokens = tokens_ref[camera_rows(1 - odd, rows), :]
    write_finished(1, pieces, tokens, out_weight_ref, info_ref, mixed_ref, payload_ref)


def outer_kernel(
    early_ref, late_ref, weight_ref, info_ref, query_ref, part_ref, tokens_ref, out_weight_ref, inner_ref, mixed_ref,
    payload_ref, value_ref,
):
    rows = mixed_ref.shape[0]
    early = is_early()
    far = jnp.where(early, sent_rows(early_ref), sent_rows(late_ref))
    far_count = jnp.where(early, sent_count(early_ref), sent_count(late_ref))
    keys = padded_keys(dot_nt(far, weight_ref[INNER : 2 * INNER, :]))
    keys = with_side(keys, info_ref[0:1, :])
    value_ref[...] = rounded(dot_nt(weight_ref[2 * INNER :, :], far))
    payload_ref[inner_ref.shape[0] :] = inner_ref[...]
    bias = keys_bias(rows, far_count)
    one_rows = one_then_zeros(LANES - HEAD, rows)
    value_ones = one_then_zeros(8, rows)
    pieces = []

    def score(h):
        q = jnp.concatenate([head_rows(query_ref[:, :rows], h), one_rows], axis=0).astype(jnp.bfloat16)
        return dot_nn(key_window(keys, h, bias), q)

    def rest(h, scores):
        part = part_ref[h]
        before = part[HEAD + 1 : HEAD + 2, :]
        highest = jnp.maximum(jnp.max(scores, axis=0, keepdims=True), before)
        expo = jnp.exp2((scores - highest) * COEF).astype(jnp.bfloat16)
        v = jnp.concatenate([head_rows(value_ref[...], h), value_ones], axis=0).astype(jnp.bfloat16)
        summed = part * jnp.exp2((before - highest) * COEF) + dot_nn(v, expo)
        pieces.append(summed[:HEAD] * (1.0 / summed[HEAD : HEAD + 1]))

    staggered(list(range(HEADS)), score, rest, HEADS)
    tokens = tokens_ref[camera_rows(cam_is_odd(), rows), :]
    write_finished(0, pieces, tokens, out_weight_ref, info_ref, mixed_ref, payload_ref)


def time_kernel(frames, payload_ref, weight_ref, out_ref, query_ref, value_ref):
    size = frames * PLACES
    rows = GROUPS * size
    model = weight_ref.shape[1]
    normed = jnp.concatenate(
        [payload_ref[:, :, g * model : (g + 1) * model].reshape(size, model) for g in range(GROUPS)], axis=0
    )
    keys = padded_keys(dot_nt(normed, weight_ref[INNER : 2 * INNER, :]))
    query_ref[...] = rounded(dot_nt(weight_ref[:INNER, :], normed))
    value_ref[...] = rounded(dot_nt(weight_ref[2 * INNER :, :], normed))
    valid = payload_ref[:, :, GROUPS * model :].reshape(size, LANES).astype(jnp.float32)
    lane = lax.broadcasted_iota(jnp.int32, (size, LANES), 1)
    key = lax.broadcasted_iota(jnp.int32, (size, LANES), 0)
    key_masks = []
    for g in range(GROUPS):
        first = g * (LANES // GROUPS)
        invalid = valid[:, first : first + 1] < 0.5
        key_mask = jnp.where(
            lane < frames,
            jnp.where(jnp.logical_and(invalid, lane != key // PLACES), -BIG, 0.0),
            jnp.where(lane - frames == key % PLACES, 1.0, 0.0),
        )
        key_masks.append(key_mask.astype(jnp.bfloat16))
    entry = lax.broadcasted_iota(jnp.int32, (LANES, size), 0)
    query = lax.broadcasted_iota(jnp.int32, (LANES, size), 1)
    query_mask = jnp.where(
        entry < frames,
        jnp.where(entry == query // PLACES, 1.0, 0.0),
        jnp.where(jnp.logical_and(entry < frames + PLACES, entry - frames != query % PLACES), -BIG, 0.0),
    ).astype(jnp.bfloat16)
    zero_rows = jnp.zeros((LANES - HEAD, size), jnp.float32)
    value_ones = one_then_zeros(8, size)
    pieces = [[] for _ in range(GROUPS)]

    def score(item):
        h, g = item
        here = slice(g * size, (g + 1) * size)
        q = jnp.concatenate([head_rows(query_ref[:, here], h), zero_rows], axis=0).astype(jnp.bfloat16)
        return dot_nn(
            jnp.concatenate([key_window(keys[here], h, None), key_masks[g]], axis=1),
            jnp.concatenate([q, query_mask], axis=0),
        )

    def rest(item, scores):
        h, g = item
        highest = jnp.max(scores, axis=0, keepdims=True)
        expo = jnp.exp2((scores - highest) * COEF).astype(jnp.bfloat16)
        v = head_rows(value_ref[:, g * size : (g + 1) * size], h)
        summed = dot_nn(jnp.concatenate([v, value_ones], axis=0).astype(jnp.bfloat16), expo)
        pieces[g].append(summed[:HEAD] * (1.0 / summed[HEAD : HEAD + 1]))

    staggered([(h, g) for g in range(GROUPS) for h in range(HEADS)], score, rest, 10)
    attended = jnp.concatenate(sum(pieces, []), axis=0).T.astype(jnp.bfloat16)
    out_ref[...] = attended.reshape(frames, PLACES, GROUPS * INNER)


def final_kernel(attended_ref, weight_ref, outer_ref, inner_ref, out_hbm, block_ref, sems):
    rows = outer_ref.shape[0]
    size = rows // GROUPS
    chunks = size // PLACES
    half = GROUPS // 2
    odd = cam_is_odd()
    copies = []
    for i, (cam, mixed_ref) in enumerate(((odd, outer_ref), (1 - odd, inner_ref))):
        here = slice(i * chunks, (i + 1) * chunks)
        blocks = [
            attended_ref[here, :, g * INNER : (g + 1) * INNER].reshape(size, INNER) for g in range(GROUPS)
        ]
        for part in range(2):
            slot = len(copies)
            start = part * half * size
            attended = jnp.concatenate(blocks[part * half : (part + 1) * half], axis=0)
            result = dot_nn(attended, weight_ref[...])
            result = result + mixed_ref[start : start + half * size, :].astype(jnp.float32)
            block_ref[slot] = result.astype(jnp.bfloat16)
            there = pl.ds(pl.multiple_of(cam * rows + start, half * size), half * size)
            copies.append(pltpu.make_async_copy(block_ref.at[slot], out_hbm.at[there], sems.at[slot]))
            copies[-1].start()
    for copy in copies:
        copy.wait()


SMEM = pl.BlockSpec(memory_space=pltpu.SMEM)
VMEM = pl.BlockSpec(memory_space=pltpu.VMEM)
ANY = pl.BlockSpec(memory_space=pl.ANY)


def kernel_call(body, ins, outs, scratch, mib, flops, nbytes, out_space=VMEM):
    return pl.pallas_call(
        body,
        out_shape=outs,
        in_specs=ins,
        out_specs=[out_space] * len(outs),
        scratch_shapes=scratch,
        compiler_params=pltpu.CompilerParams(vmem_limit_bytes=mib * MIB),
        cost_estimate=pl.CostEstimate(flops=flops, bytes_accessed=nbytes, transcendentals=0),
    )


def shards(tokens, counts, neighbours, side_keys, cross_qkv, cross_out, time_qkv, time_out):
    cam_here, frames_here, token_count, model = tokens.shape
    cameras = cam_here * lax.axis_size("cam")
    frames = lax.axis_size("frame")
    rows = cam_here * token_count
    bf16 = jnp.bfloat16
    spread = functools.partial(jax.ShapeDtypeStruct, dtype=bf16)

    flat = tokens.reshape(rows, model)
    payload_lanes = GROUPS * model + LANES
    own_counts = counts.reshape(1, cam_here)
    cross_t, time_t = cross_qkv.T, time_qkv.T
    inside_pairs, early_pairs, late_pairs = exchange_pairs(lax.axis_size("cam"))
    sent = (token_count // 4 + 1, 4, model)

    outer, inner = kernel_call(
        norm_kernel, [SMEM, VMEM], [spread(sent)] * 2, [], 16, 6_000_000_000, 2_400_000
    )(own_counts, flat)
    early_far = lax.ppermute(outer, "cam", early_pairs)
    inner_far = lax.ppermute(inner, "cam", inside_pairs)

    query, part, info, mixed_inner, payload_inner = kernel_call(
        functools.partial(local_kernel, cameras),
        [SMEM, SMEM] + [VMEM] * 7,
        [
            jax.ShapeDtypeStruct((INNER, rows), jnp.float32),
            jax.ShapeDtypeStruct((HEADS, HEAD + 8, token_count), jnp.float32),
            jax.ShapeDtypeStruct((8, KEY_LANES), jnp.float32),
            spread((token_count, model)),
            spread((frames // 2, PLACES, payload_lanes)),
        ],
        [pltpu.VMEM((INNER, rows + token_count), jnp.float32)],
        36,
        8_000_000_000,
        20_000_000,
    )(own_counts, neighbours, outer, inner, inner_far, cross_t, side_keys, flat, cross_out)
    outer, payload_inner = lax.optimization_barrier((outer, payload_inner))
    late_far = lax.ppermute(outer, "cam", late_pairs)
    mixed_outer, payload = kernel_call(
        outer_kernel,
        [VMEM] * 9,
        [spread((token_count, model)), spread((frames, PLACES, payload_lanes))],
        [pltpu.VMEM((INNER, token_count), jnp.float32)],
        32,
        2_500_000_000,
        8_000_000,
    )(early_far, late_far, cross_t, info, query, part, flat, cross_out, payload_inner)

    arrived = to_owners(payload)
    (attended,) = kernel_call(
        functools.partial(time_kernel, frames),
        [VMEM] * 2,
        [spread((frames, PLACES, GROUPS * INNER))],
        [pltpu.VMEM((INNER, rows), jnp.float32)] * 2,
        32,
        6_000_000_000,
        10_000_000,
    )(arrived, time_t)
    returned = to_owners(attended)
    (out,) = kernel_call(
        final_kernel,
        [VMEM] * 4,
        [spread((rows, model))],
        [pltpu.VMEM((4, rows // 4, model), bf16), pltpu.SemaphoreType.DMA((4,))],
        32,
        700_000_000,
        4_000_000,
        ANY,
    )(returned, time_out, mixed_outer, mixed_inner)
    return out.reshape(tokens.shape)


def solution(mesh):
    return jax.shard_map(
        shards,
        mesh=mesh,
        in_specs=(
            P("cam", "frame", None, None),
            P("cam", "frame"),
            P("cam", None),
            P(),
            P(),
            P(),
            P(),
            P(),
        ),
        out_specs=P("cam", "frame", None, None),
        check_vma=False,
    )
```

```python
import functools
import math

import jax
import jax.numpy as jnp
from jax import lax
from jax.experimental import pallas as pl
from jax.experimental.pallas import tpu as pltpu
from jax.sharding import PartitionSpec as P

HEADS = 8
HEAD = 72
INNER = HEADS * HEAD
EPS = 1e-06
ROW_TOKENS = 64
BIG = 1e30
COEF = HEAD ** (-0.5) * math.log2(math.e)
LANES = 128
KEY_LANES = 640
PLACES = 2
GROUPS = 4
MIB = 1 << 20


def to_owners(x):
    return lax.all_to_all(x, "frame", split_axis=0, concat_axis=0, tiled=True)


def cam_is_odd():
    return lax.rem(lax.axis_index("cam"), 2)


def exchange_pairs(peers):
    inside, early, late = [], [], []
    for i in range(0, peers, 2):
        inside += [(i, i + 1), (i + 1, i)]
        last = (i + peers - 1) % peers
        (early if (i // 2) % 2 else late).extend([(last, i), (i, last)])
    return inside, early, late


def is_early():
    peers = lax.axis_size("cam")
    return lax.rem(lax.rem(lax.axis_index("cam") + 1, peers) // 2, 2) == 1


def dot_nt(a, b):
    return lax.dot_general(a, b, (((1,), (1,)), ((), ())), preferred_element_type=jnp.float32)


def dot_nn(a, b):
    return lax.dot_general(a, b, (((1,), (0,)), ((), ())), preferred_element_type=jnp.float32)


def normalize(values):
    values = values.astype(jnp.float32)
    mean = jnp.mean(values, axis=-1, keepdims=True)
    centred = values - mean
    variance = jnp.mean(centred * centred, axis=-1, keepdims=True)
    return (centred * lax.rsqrt(variance + EPS)).astype(jnp.bfloat16)


def keys_bias(rows, count):
    position = lax.broadcasted_iota(jnp.int32, (rows, LANES), 0).astype(jnp.float32)
    return jnp.where(position < ROW_TOKENS * count, 0.0, -BIG).astype(jnp.bfloat16)


def key_window(keys, head, bias):
    window = keys[:, head * HEAD : head * HEAD + LANES]
    lane = lax.broadcasted_iota(jnp.int32, window.shape, 1)
    window = jnp.where(lane < HEAD, window, jnp.zeros_like(window))
    return window if bias is None else jnp.where(lane == HEAD, bias, window)


def one_then_zeros(rows, columns):
    return jnp.where(lax.broadcasted_iota(jnp.int32, (rows, columns), 0) == 0, 1.0, 0.0)


def head_rows(x, head):
    return x[head * HEAD : (head + 1) * HEAD, :]


def rounded(x):
    return x.astype(jnp.bfloat16).astype(jnp.float32)


def padded_keys(keys):
    fill = jnp.zeros((keys.shape[0], KEY_LANES - keys.shape[1]), jnp.float32)
    return jnp.concatenate([keys, fill], axis=1).astype(jnp.bfloat16)


def with_side(keys, side):
    return (keys.astype(jnp.float32) + side).astype(jnp.bfloat16)


def side_row(side, neighbours_ref, cam, lower, cameras, cam_here):
    camera = lax.axis_index("cam") * cam_here + cam
    first_lower = neighbours_ref[cam, 0] == lax.rem(camera + cameras - 1, cameras)
    return jnp.where(first_lower == lower, side[0:1, :], side[1:2, :])


def staggered(items, score, rest, ahead):
    scores = [score(item) for item in items[:ahead]]
    for i, item in enumerate(items):
        if i + ahead < len(items):
            scores.append(score(items[i + ahead]))
        rest(item, scores[i])
        scores[i] = None


def camera_rows(cam, rows):
    return pl.ds(pl.multiple_of(cam * rows, rows), rows)


def norm_kernel(counts_ref, tokens_ref, outer_ref, inner_ref):
    rows = tokens_ref.shape[0] // 2
    odd = cam_is_odd()
    for cam, out_ref in ((odd, outer_ref), (1 - odd, inner_ref)):
        last, *block = out_ref.shape
        last -= 1
        out_ref[:last] = normalize(tokens_ref[camera_rows(cam, rows), :]).reshape(last, *block)
        count = counts_ref[0, cam].astype(jnp.float32)
        out_ref[last:] = jnp.full((1, *block), count, jnp.float32).astype(jnp.bfloat16)


def sent_rows(ref):
    blocks, size, width = ref.shape
    return ref[: blocks - 1].reshape((blocks - 1) * size, width)


def sent_count(ref):
    return ref[ref.shape[0] - 1, :, :LANES].astype(jnp.float32)[:1]


def write_finished(i, pieces, tokens, out_weight_ref, info_ref, mixed_ref, payload_ref):
    attended = jnp.concatenate(pieces, axis=0).T.astype(jnp.bfloat16)
    mixed = (dot_nn(attended, out_weight_ref[...]) + tokens.astype(jnp.float32)).astype(jnp.bfloat16)
    rows, width = mixed.shape
    mixed_ref[...] = mixed
    normed = normalize(mixed)
    size = rows // GROUPS
    chunks = size // PLACES
    for g in range(GROUPS):
        block = normed[g * size : (g + 1) * size].reshape(chunks, PLACES, width)
        payload_ref[:chunks, :, g * width : (g + 1) * width] = block
    group = lax.broadcasted_iota(jnp.int32, (size, LANES), 1) // (LANES // GROUPS)
    position = lax.broadcasted_iota(jnp.int32, (size, LANES), 0) + group * size
    valid = position.astype(jnp.float32) < ROW_TOKENS * info_ref[2 + i : 3 + i, :LANES]
    valid = jnp.where(valid, 1.0, 0.0).astype(jnp.bfloat16)
    payload_ref[:chunks, :, GROUPS * width :] = valid.reshape(chunks, PLACES, LANES)


def local_kernel(
    cameras, counts_ref, neighbours_ref, outer_ref, inner_ref, far_ref, weight_ref, side_ref, tokens_ref, out_weight_ref,
    query_ref, part_ref, info_ref, mixed_ref, payload_ref, value_ref,
):
    rows = mixed_ref.shape[0]
    odd = cam_is_odd()
    cams = (odd, 1 - odd)
    normed = jnp.concatenate([sent_rows(ref) for ref in (outer_ref, inner_ref, far_ref)], axis=0)
    keys = padded_keys(dot_nt(normed, weight_ref[INNER : 2 * INNER, :]))
    query_ref[...] = rounded(dot_nt(weight_ref[:INNER, :], normed[: 2 * rows]))
    value_ref[...] = rounded(dot_nt(weight_ref[2 * INNER :, :], normed))
    sides = jnp.concatenate(
        [side_ref[...].astype(jnp.float32), jnp.zeros((2, KEY_LANES - INNER), jnp.float32)], axis=1
    )
    far_sides = [side_row(sides, neighbours_ref, cam, cam == 0, cameras, 2) for cam in cams]
    near_sides = [side_row(sides, neighbours_ref, cam, cam == 1, cameras, 2) for cam in cams]
    counts = [counts_ref[0, cam].astype(jnp.float32) for cam in cams]
    info_ref[0:1, :] = far_sides[0]
    info_ref[1:2, :] = far_sides[1]
    for i in range(2):
        info_ref[2 + i : 3 + i, :] = jnp.full((1, KEY_LANES), counts[i], jnp.float32)
    info_ref[4:, :] = jnp.zeros((info_ref.shape[0] - 4, KEY_LANES), jnp.float32)
    biases = [keys_bias(rows, count) for count in counts]
    far_bias = keys_bias(rows, sent_count(far_ref))
    one_rows = one_then_zeros(LANES - HEAD, rows)
    value_ones = one_then_zeros(8, 3 * rows)
    outer, inner, far = (slice(i * rows, (i + 1) * rows) for i in range(3))
    kept = (
        (
            outer,
            (outer, inner),
            jnp.concatenate([keys[outer], with_side(keys[inner], near_sides[0])], axis=0),
            jnp.concatenate([biases[0], biases[1]], axis=0),
        ),
        (
            inner,
            (inner, outer, far),
            jnp.concatenate(
                [keys[inner], with_side(keys[outer], near_sides[1]), with_side(keys[far], far_sides[1])], axis=0
            ),
            jnp.concatenate([biases[1], biases[0], far_bias], axis=0),
        ),
    )
    pieces = []

    def score(item):
        i, h = item
        own, _, k_all, bias = kept[i]
        q = jnp.concatenate([head_rows(query_ref[:, own], h), one_rows], axis=0).astype(jnp.bfloat16)
        return dot_nn(key_window(k_all, h, bias), q)

    def rest(item, scores):
        i, h = item
        blocks = kept[i][1]
        highest = jnp.max(scores, axis=0, keepdims=True)
        expo = jnp.exp2((scores - highest) * COEF).astype(jnp.bfloat16)
        v = jnp.concatenate([head_rows(value_ref[:, block], h) for block in blocks], axis=1)
        v = jnp.concatenate([v, value_ones[:, : v.shape[1]]], axis=0).astype(jnp.bfloat16)
        summed = dot_nn(v, expo)
        if i == 0:
            row = lax.broadcasted_iota(jnp.int32, summed.shape, 0)
            part_ref[h] = jnp.where(row == HEAD + 1, highest, summed)
        else:
            pieces.append(summed[:HEAD] * (1.0 / summed[HEAD : HEAD + 1]))

    staggered([(i, h) for i in (1, 0) for h in range(HEADS)], score, rest, 8)
    tokens = tokens_ref[camera_rows(1 - odd, rows), :]
    write_finished(1, pieces, tokens, out_weight_ref, info_ref, mixed_ref, payload_ref)


def outer_kernel(
    early_ref, late_ref, weight_ref, info_ref, query_ref, part_ref, tokens_ref, out_weight_ref, inner_ref, mixed_ref,
    payload_ref, value_ref,
):
    rows = mixed_ref.shape[0]
    early = is_early()
    far = jnp.where(early, sent_rows(early_ref), sent_rows(late_ref))
    far_count = jnp.where(early, sent_count(early_ref), sent_count(late_ref))
    keys = padded_keys(dot_nt(far, weight_ref[INNER : 2 * INNER, :]))
    keys = with_side(keys, info_ref[0:1, :])
    value_ref[...] = rounded(dot_nt(weight_ref[2 * INNER :, :], far))
    payload_ref[inner_ref.shape[0] :] = inner_ref[...]
    bias = keys_bias(rows, far_count)
    one_rows = one_then_zeros(LANES - HEAD, rows)
    value_ones = one_then_zeros(8, rows)
    pieces = []

    def score(h):
        q = jnp.concatenate([head_rows(query_ref[:, :rows], h), one_rows], axis=0).astype(jnp.bfloat16)
        return dot_nn(key_window(keys, h, bias), q)

    def rest(h, scores):
        part = part_ref[h]
        before = part[HEAD + 1 : HEAD + 2, :]
        highest = jnp.maximum(jnp.max(scores, axis=0, keepdims=True), before)
        expo = jnp.exp2((scores - highest) * COEF).astype(jnp.bfloat16)
        v = jnp.concatenate([head_rows(value_ref[...], h), value_ones], axis=0).astype(jnp.bfloat16)
        summed = part * jnp.exp2((before - highest) * COEF) + dot_nn(v, expo)
        pieces.append(summed[:HEAD] * (1.0 / summed[HEAD : HEAD + 1]))

    staggered(list(range(HEADS)), score, rest, HEADS)
    tokens = tokens_ref[camera_rows(cam_is_odd(), rows), :]
    write_finished(0, pieces, tokens, out_weight_ref, info_ref, mixed_ref, payload_ref)


def time_kernel(frames, payload_ref, weight_ref, out_ref, query_ref, value_ref):
    size = frames * PLACES
    rows = GROUPS * size
    model = weight_ref.shape[1]
    normed = jnp.concatenate(
        [payload_ref[:, :, g * model : (g + 1) * model].reshape(size, model) for g in range(GROUPS)], axis=0
    )
    keys = padded_keys(dot_nt(normed, weight_ref[INNER : 2 * INNER, :]))
    query_ref[...] = rounded(dot_nt(weight_ref[:INNER, :], normed))
    value_ref[...] = rounded(dot_nt(weight_ref[2 * INNER :, :], normed))
    valid = payload_ref[:, :, GROUPS * model :].reshape(size, LANES).astype(jnp.float32)
    lane = lax.broadcasted_iota(jnp.int32, (size, LANES), 1)
    key = lax.broadcasted_iota(jnp.int32, (size, LANES), 0)
    key_masks = []
    for g in range(GROUPS):
        first = g * (LANES // GROUPS)
        invalid = valid[:, first : first + 1] < 0.5
        key_mask = jnp.where(
            lane < frames,
            jnp.where(jnp.logical_and(invalid, lane != key // PLACES), -BIG, 0.0),
            jnp.where(lane - frames == key % PLACES, 1.0, 0.0),
        )
        key_masks.append(key_mask.astype(jnp.bfloat16))
    entry = lax.broadcasted_iota(jnp.int32, (LANES, size), 0)
    query = lax.broadcasted_iota(jnp.int32, (LANES, size), 1)
    query_mask = jnp.where(
        entry < frames,
        jnp.where(entry == query // PLACES, 1.0, 0.0),
        jnp.where(jnp.logical_and(entry < frames + PLACES, entry - frames != query % PLACES), -BIG, 0.0),
    ).astype(jnp.bfloat16)
    zero_rows = jnp.zeros((LANES - HEAD, size), jnp.float32)
    value_ones = one_then_zeros(8, size)
    pieces = [[] for _ in range(GROUPS)]

    def score(item):
        h, g = item
        here = slice(g * size, (g + 1) * size)
        q = jnp.concatenate([head_rows(query_ref[:, here], h), zero_rows], axis=0).astype(jnp.bfloat16)
        return dot_nn(
            jnp.concatenate([key_window(keys[here], h, None), key_masks[g]], axis=1),
            jnp.concatenate([q, query_mask], axis=0),
        )

    def rest(item, scores):
        h, g = item
        highest = jnp.max(scores, axis=0, keepdims=True)
        expo = jnp.exp2((scores - highest) * COEF).astype(jnp.bfloat16)
        v = head_rows(value_ref[:, g * size : (g + 1) * size], h)
        summed = dot_nn(jnp.concatenate([v, value_ones], axis=0).astype(jnp.bfloat16), expo)
        pieces[g].append(summed[:HEAD] * (1.0 / summed[HEAD : HEAD + 1]))

    staggered([(h, g) for g in range(GROUPS) for h in range(HEADS)], score, rest, 10)
    attended = jnp.concatenate(sum(pieces, []), axis=0).T.astype(jnp.bfloat16)
    out_ref[...] = attended.reshape(frames, PLACES, GROUPS * INNER)


def final_kernel(attended_ref, weight_ref, outer_ref, inner_ref, out_hbm, block_ref, sems):
    rows = outer_ref.shape[0]
    size = rows // GROUPS
    chunks = size // PLACES
    half = GROUPS // 2
    odd = cam_is_odd()
    copies = []
    for i, (cam, mixed_ref) in enumerate(((odd, outer_ref), (1 - odd, inner_ref))):
        here = slice(i * chunks, (i + 1) * chunks)
        blocks = [
            attended_ref[here, :, g * INNER : (g + 1) * INNER].reshape(size, INNER) for g in range(GROUPS)
        ]
        for part in range(2):
            slot = len(copies)
            start = part * half * size
            attended = jnp.concatenate(blocks[part * half : (part + 1) * half], axis=0)
            result = dot_nn(attended, weight_ref[...])
            result = result + mixed_ref[start : start + half * size, :].astype(jnp.float32)
            block_ref[slot] = result.astype(jnp.bfloat16)
            there = pl.ds(pl.multiple_of(cam * rows + start, half * size), half * size)
            copies.append(pltpu.make_async_copy(block_ref.at[slot], out_hbm.at[there], sems.at[slot]))
            copies[-1].start()
    for copy in copies:
        copy.wait()


SMEM = pl.BlockSpec(memory_space=pltpu.SMEM)
VMEM = pl.BlockSpec(memory_space=pltpu.VMEM)
ANY = pl.BlockSpec(memory_space=pl.ANY)


def kernel_call(body, ins, outs, scratch, mib, flops, nbytes, out_space=VMEM):
    return pl.pallas_call(
        body,
        out_shape=outs,
        in_specs=ins,
        out_specs=[out_space] * len(outs),
        scratch_shapes=scratch,
        compiler_params=pltpu.CompilerParams(vmem_limit_bytes=mib * MIB),
        cost_estimate=pl.CostEstimate(flops=flops, bytes_accessed=nbytes, transcendentals=0),
    )


def shards(tokens, counts, neighbours, side_keys, cross_qkv, cross_out, time_qkv, time_out):
    cam_here, frames_here, token_count, model = tokens.shape
    cameras = cam_here * lax.axis_size("cam")
    frames = lax.axis_size("frame")
    rows = cam_here * token_count
    bf16 = jnp.bfloat16
    spread = functools.partial(jax.ShapeDtypeStruct, dtype=bf16)

    flat = tokens.reshape(rows, model)
    payload_lanes = GROUPS * model + LANES
    own_counts = counts.reshape(1, cam_here)
    cross_t, time_t = cross_qkv.T, time_qkv.T
    inside_pairs, early_pairs, late_pairs = exchange_pairs(lax.axis_size("cam"))
    sent = (token_count // 4 + 1, 4, model)

    outer, inner = kernel_call(
        norm_kernel, [SMEM, VMEM], [spread(sent)] * 2, [], 16, 6_000_000_000, 2_400_000
    )(own_counts, flat)
    early_far = lax.ppermute(outer, "cam", early_pairs)
    inner_far = lax.ppermute(inner, "cam", inside_pairs)

    query, part, info, mixed_inner, payload_inner = kernel_call(
        functools.partial(local_kernel, cameras),
        [SMEM, SMEM] + [VMEM] * 7,
        [
            jax.ShapeDtypeStruct((INNER, rows), jnp.float32),
            jax.ShapeDtypeStruct((HEADS, HEAD + 8, token_count), jnp.float32),
            jax.ShapeDtypeStruct((8, KEY_LANES), jnp.float32),
            spread((token_count, model)),
            spread((frames // 2, PLACES, payload_lanes)),
        ],
        [pltpu.VMEM((INNER, rows + token_count), jnp.float32)],
        36,
        8_000_000_000,
        20_000_000,
    )(own_counts, neighbours, outer, inner, inner_far, cross_t, side_keys, flat, cross_out)
    outer, payload_inner = lax.optimization_barrier((outer, payload_inner))
    late_far = lax.ppermute(outer, "cam", late_pairs)
    mixed_outer, payload = kernel_call(
        outer_kernel,
        [VMEM] * 9,
        [spread((token_count, model)), spread((frames, PLACES, payload_lanes))],
        [pltpu.VMEM((INNER, token_count), jnp.float32)],
        32,
        2_500_000_000,
        8_000_000,
    )(early_far, late_far, cross_t, info, query, part, flat, cross_out, payload_inner)

    arrived = to_owners(payload)
    (attended,) = kernel_call(
        functools.partial(time_kernel, frames),
        [VMEM] * 2,
        [spread((frames, PLACES, GROUPS * INNER))],
        [pltpu.VMEM((INNER, rows), jnp.float32)] * 2,
        32,
        6_000_000_000,
        10_000_000,
    )(arrived, time_t)
    returned = to_owners(attended)
    (out,) = kernel_call(
        final_kernel,
        [VMEM] * 4,
        [spread((rows, model))],
        [pltpu.VMEM((4, rows // 4, model), bf16), pltpu.SemaphoreType.DMA((4,))],
        32,
        700_000_000,
        4_000_000,
        ANY,
    )(returned, time_out, mixed_outer, mixed_inner)
    return out.reshape(tokens.shape)


def solution(mesh):
    return jax.shard_map(
        shards,
        mesh=mesh,
        in_specs=(
            P("cam", "frame", None, None),
            P("cam", "frame"),
            P("cam", None),
            P(),
            P(),
            P(),
            P(),
            P(),
        ),
        out_specs=P("cam", "frame", None, None),
        check_vma=False,
    )
```

```python
import functools
import math

import jax
import jax.numpy as jnp
from jax import lax
from jax.experimental import pallas as pl
from jax.experimental.pallas import tpu as pltpu
from jax.sharding import PartitionSpec as P

HEADS = 8
HEAD = 72
INNER = HEADS * HEAD
EPS = 1e-06
ROW_TOKENS = 64
BIG = 1e30
COEF = HEAD ** (-0.5) * math.log2(math.e)
LANES = 128
KEY_LANES = 640
PLACES = 2
GROUPS = 4
MIB = 1 << 20


def to_owners(x):
    return lax.all_to_all(x, "frame", split_axis=0, concat_axis=0, tiled=True)


def cam_is_odd():
    return lax.rem(lax.axis_index("cam"), 2)


def exchange_pairs(peers):
    inside, early, late = [], [], []
    for i in range(0, peers, 2):
        inside += [(i, i + 1), (i + 1, i)]
        last = (i + peers - 1) % peers
        (early if (i // 2) % 2 else late).extend([(last, i), (i, last)])
    return inside, early, late


def is_early():
    peers = lax.axis_size("cam")
    return lax.rem(lax.rem(lax.axis_index("cam") + 1, peers) // 2, 2) == 1


def dot_nt(a, b):
    return lax.dot_general(a, b, (((1,), (1,)), ((), ())), preferred_element_type=jnp.float32)


def dot_nn(a, b):
    return lax.dot_general(a, b, (((1,), (0,)), ((), ())), preferred_element_type=jnp.float32)


def normalize(values):
    values = values.astype(jnp.float32)
    mean = jnp.mean(values, axis=-1, keepdims=True)
    centred = values - mean
    variance = jnp.mean(centred * centred, axis=-1, keepdims=True)
    return (centred * lax.rsqrt(variance + EPS)).astype(jnp.bfloat16)


def keys_bias(rows, count):
    position = lax.broadcasted_iota(jnp.int32, (rows, LANES), 0).astype(jnp.float32)
    return jnp.where(position < ROW_TOKENS * count, 0.0, -BIG).astype(jnp.bfloat16)


def key_window(keys, head, bias):
    window = keys[:, head * HEAD : head * HEAD + LANES]
    lane = lax.broadcasted_iota(jnp.int32, window.shape, 1)
    window = jnp.where(lane < HEAD, window, jnp.zeros_like(window))
    return window if bias is None else jnp.where(lane == HEAD, bias, window)


def one_then_zeros(rows, columns):
    return jnp.where(lax.broadcasted_iota(jnp.int32, (rows, columns), 0) == 0, 1.0, 0.0)


def head_rows(x, head):
    return x[head * HEAD : (head + 1) * HEAD, :]


def rounded(x):
    return x.astype(jnp.bfloat16).astype(jnp.float32)


def padded_keys(keys):
    fill = jnp.zeros((keys.shape[0], KEY_LANES - keys.shape[1]), jnp.float32)
    return jnp.concatenate([keys, fill], axis=1).astype(jnp.bfloat16)


def with_side(keys, side):
    return (keys.astype(jnp.float32) + side).astype(jnp.bfloat16)


def side_row(side, neighbours_ref, cam, lower, cameras, cam_here):
    camera = lax.axis_index("cam") * cam_here + cam
    first_lower = neighbours_ref[cam, 0] == lax.rem(camera + cameras - 1, cameras)
    return jnp.where(first_lower == lower, side[0:1, :], side[1:2, :])


def staggered(items, score, rest, ahead):
    scores = [score(item) for item in items[:ahead]]
    for i, item in enumerate(items):
        if i + ahead < len(items):
            scores.append(score(items[i + ahead]))
        rest(item, scores[i])
        scores[i] = None


def camera_rows(cam, rows):
    return pl.ds(pl.multiple_of(cam * rows, rows), rows)


def norm_kernel(counts_ref, tokens_ref, outer_ref, inner_ref):
    rows = tokens_ref.shape[0] // 2
    odd = cam_is_odd()
    for cam, out_ref in ((odd, outer_ref), (1 - odd, inner_ref)):
        last, *block = out_ref.shape
        last -= 1
        out_ref[:last] = normalize(tokens_ref[camera_rows(cam, rows), :]).reshape(last, *block)
        count = counts_ref[0, cam].astype(jnp.float32)
        out_ref[last:] = jnp.full((1, *block), count, jnp.float32).astype(jnp.bfloat16)


def sent_rows(ref):
    blocks, size, width = ref.shape
    return ref[: blocks - 1].reshape((blocks - 1) * size, width)


def sent_count(ref):
    return ref[ref.shape[0] - 1, :, :LANES].astype(jnp.float32)[:1]


def write_finished(i, pieces, tokens, out_weight_ref, info_ref, mixed_ref, payload_ref):
    attended = jnp.concatenate(pieces, axis=0).T.astype(jnp.bfloat16)
    mixed = (dot_nn(attended, out_weight_ref[...]) + tokens.astype(jnp.float32)).astype(jnp.bfloat16)
    rows, width = mixed.shape
    mixed_ref[...] = mixed
    normed = normalize(mixed)
    size = rows // GROUPS
    chunks = size // PLACES
    for g in range(GROUPS):
        block = normed[g * size : (g + 1) * size].reshape(chunks, PLACES, width)
        payload_ref[:chunks, :, g * width : (g + 1) * width] = block
    group = lax.broadcasted_iota(jnp.int32, (size, LANES), 1) // (LANES // GROUPS)
    position = lax.broadcasted_iota(jnp.int32, (size, LANES), 0) + group * size
    valid = position.astype(jnp.float32) < ROW_TOKENS * info_ref[2 + i : 3 + i, :LANES]
    valid = jnp.where(valid, 1.0, 0.0).astype(jnp.bfloat16)
    payload_ref[:chunks, :, GROUPS * width :] = valid.reshape(chunks, PLACES, LANES)


def local_kernel(
    cameras, counts_ref, neighbours_ref, outer_ref, inner_ref, far_ref, weight_ref, side_ref, tokens_ref, out_weight_ref,
    query_ref, part_ref, info_ref, mixed_ref, payload_ref, value_ref,
):
    rows = mixed_ref.shape[0]
    odd = cam_is_odd()
    cams = (odd, 1 - odd)
    normed = jnp.concatenate([sent_rows(ref) for ref in (outer_ref, inner_ref, far_ref)], axis=0)
    keys = padded_keys(dot_nt(normed, weight_ref[INNER : 2 * INNER, :]))
    query_ref[...] = rounded(dot_nt(weight_ref[:INNER, :], normed[: 2 * rows]))
    value_ref[...] = rounded(dot_nt(weight_ref[2 * INNER :, :], normed))
    sides = jnp.concatenate(
        [side_ref[...].astype(jnp.float32), jnp.zeros((2, KEY_LANES - INNER), jnp.float32)], axis=1
    )
    far_sides = [side_row(sides, neighbours_ref, cam, cam == 0, cameras, 2) for cam in cams]
    near_sides = [side_row(sides, neighbours_ref, cam, cam == 1, cameras, 2) for cam in cams]
    counts = [counts_ref[0, cam].astype(jnp.float32) for cam in cams]
    info_ref[0:1, :] = far_sides[0]
    info_ref[1:2, :] = far_sides[1]
    for i in range(2):
        info_ref[2 + i : 3 + i, :] = jnp.full((1, KEY_LANES), counts[i], jnp.float32)
    info_ref[4:, :] = jnp.zeros((info_ref.shape[0] - 4, KEY_LANES), jnp.float32)
    biases = [keys_bias(rows, count) for count in counts]
    far_bias = keys_bias(rows, sent_count(far_ref))
    one_rows = one_then_zeros(LANES - HEAD, rows)
    value_ones = one_then_zeros(8, 3 * rows)
    outer, inner, far = (slice(i * rows, (i + 1) * rows) for i in range(3))
    kept = (
        (
            outer,
            (outer, inner),
            jnp.concatenate([keys[outer], with_side(keys[inner], near_sides[0])], axis=0),
            jnp.concatenate([biases[0], biases[1]], axis=0),
        ),
        (
            inner,
            (inner, outer, far),
            jnp.concatenate(
                [keys[inner], with_side(keys[outer], near_sides[1]), with_side(keys[far], far_sides[1])], axis=0
            ),
            jnp.concatenate([biases[1], biases[0], far_bias], axis=0),
        ),
    )
    pieces = []

    def score(item):
        i, h = item
        own, _, k_all, bias = kept[i]
        q = jnp.concatenate([head_rows(query_ref[:, own], h), one_rows], axis=0).astype(jnp.bfloat16)
        return dot_nn(key_window(k_all, h, bias), q)

    def rest(item, scores):
        i, h = item
        blocks = kept[i][1]
        highest = jnp.max(scores, axis=0, keepdims=True)
        expo = jnp.exp2((scores - highest) * COEF).astype(jnp.bfloat16)
        v = jnp.concatenate([head_rows(value_ref[:, block], h) for block in blocks], axis=1)
        v = jnp.concatenate([v, value_ones[:, : v.shape[1]]], axis=0).astype(jnp.bfloat16)
        summed = dot_nn(v, expo)
        if i == 0:
            row = lax.broadcasted_iota(jnp.int32, summed.shape, 0)
            part_ref[h] = jnp.where(row == HEAD + 1, highest, summed)
        else:
            pieces.append(summed[:HEAD] * (1.0 / summed[HEAD : HEAD + 1]))
            if h == HEADS - 1:
                tokens = tokens_ref[camera_rows(1 - odd, rows), :]
                write_finished(1, pieces, tokens, out_weight_ref, info_ref, mixed_ref, payload_ref)

    staggered([(i, h) for i in (1, 0) for h in range(HEADS)], score, rest, 8)


def outer_kernel(
    early_ref, late_ref, weight_ref, info_ref, query_ref, part_ref, tokens_ref, out_weight_ref, inner_ref, mixed_ref,
    payload_ref, value_ref,
):
    rows = mixed_ref.shape[0]
    early = is_early()
    far = jnp.where(early, sent_rows(early_ref), sent_rows(late_ref))
    far_count = jnp.where(early, sent_count(early_ref), sent_count(late_ref))
    keys = padded_keys(dot_nt(far, weight_ref[INNER : 2 * INNER, :]))
    keys = with_side(keys, info_ref[0:1, :])
    value_ref[...] = rounded(dot_nt(weight_ref[2 * INNER :, :], far))
    payload_ref[inner_ref.shape[0] :] = inner_ref[...]
    bias = keys_bias(rows, far_count)
    one_rows = one_then_zeros(LANES - HEAD, rows)
    value_ones = one_then_zeros(8, rows)
    pieces = []

    def score(h):
        q = jnp.concatenate([head_rows(query_ref[:, :rows], h), one_rows], axis=0).astype(jnp.bfloat16)
        return dot_nn(key_window(keys, h, bias), q)

    def rest(h, scores):
        part = part_ref[h]
        before = part[HEAD + 1 : HEAD + 2, :]
        highest = jnp.maximum(jnp.max(scores, axis=0, keepdims=True), before)
        expo = jnp.exp2((scores - highest) * COEF).astype(jnp.bfloat16)
        v = jnp.concatenate([head_rows(value_ref[...], h), value_ones], axis=0).astype(jnp.bfloat16)
        summed = part * jnp.exp2((before - highest) * COEF) + dot_nn(v, expo)
        pieces.append(summed[:HEAD] * (1.0 / summed[HEAD : HEAD + 1]))

    staggered(list(range(HEADS)), score, rest, HEADS)
    tokens = tokens_ref[camera_rows(cam_is_odd(), rows), :]
    write_finished(0, pieces, tokens, out_weight_ref, info_ref, mixed_ref, payload_ref)


def time_kernel(frames, payload_ref, weight_ref, out_ref, query_ref, value_ref):
    size = frames * PLACES
    rows = GROUPS * size
    model = weight_ref.shape[1]
    normed = jnp.concatenate(
        [payload_ref[:, :, g * model : (g + 1) * model].reshape(size, model) for g in range(GROUPS)], axis=0
    )
    keys = padded_keys(dot_nt(normed, weight_ref[INNER : 2 * INNER, :]))
    query_ref[...] = rounded(dot_nt(weight_ref[:INNER, :], normed))
    value_ref[...] = rounded(dot_nt(weight_ref[2 * INNER :, :], normed))
    valid = payload_ref[:, :, GROUPS * model :].reshape(size, LANES).astype(jnp.float32)
    lane = lax.broadcasted_iota(jnp.int32, (size, LANES), 1)
    key = lax.broadcasted_iota(jnp.int32, (size, LANES), 0)
    key_masks = []
    for g in range(GROUPS):
        first = g * (LANES // GROUPS)
        invalid = valid[:, first : first + 1] < 0.5
        key_mask = jnp.where(
            lane < frames,
            jnp.where(jnp.logical_and(invalid, lane != key // PLACES), -BIG, 0.0),
            jnp.where(lane - frames == key % PLACES, 1.0, 0.0),
        )
        key_masks.append(key_mask.astype(jnp.bfloat16))
    entry = lax.broadcasted_iota(jnp.int32, (LANES, size), 0)
    query = lax.broadcasted_iota(jnp.int32, (LANES, size), 1)
    query_mask = jnp.where(
        entry < frames,
        jnp.where(entry == query // PLACES, 1.0, 0.0),
        jnp.where(jnp.logical_and(entry < frames + PLACES, entry - frames != query % PLACES), -BIG, 0.0),
    ).astype(jnp.bfloat16)
    zero_rows = jnp.zeros((LANES - HEAD, size), jnp.float32)
    value_ones = one_then_zeros(8, size)
    pieces = [[] for _ in range(GROUPS)]

    def score(item):
        h, g = item
        here = slice(g * size, (g + 1) * size)
        q = jnp.concatenate([head_rows(query_ref[:, here], h), zero_rows], axis=0).astype(jnp.bfloat16)
        return dot_nn(
            jnp.concatenate([key_window(keys[here], h, None), key_masks[g]], axis=1),
            jnp.concatenate([q, query_mask], axis=0),
        )

    def rest(item, scores):
        h, g = item
        highest = jnp.max(scores, axis=0, keepdims=True)
        expo = jnp.exp2((scores - highest) * COEF).astype(jnp.bfloat16)
        v = head_rows(value_ref[:, g * size : (g + 1) * size], h)
        summed = dot_nn(jnp.concatenate([v, value_ones], axis=0).astype(jnp.bfloat16), expo)
        pieces[g].append(summed[:HEAD] * (1.0 / summed[HEAD : HEAD + 1]))

    staggered([(h, g) for g in range(GROUPS) for h in range(HEADS)], score, rest, 10)
    attended = jnp.concatenate(sum(pieces, []), axis=0).T.astype(jnp.bfloat16)
    out_ref[...] = attended.reshape(frames, PLACES, GROUPS * INNER)


def final_kernel(attended_ref, weight_ref, outer_ref, inner_ref, out_hbm, block_ref, sems):
    rows = outer_ref.shape[0]
    size = rows // GROUPS
    chunks = size // PLACES
    half = GROUPS // 2
    odd = cam_is_odd()
    copies = []
    for i, (cam, mixed_ref) in enumerate(((odd, outer_ref), (1 - odd, inner_ref))):
        here = slice(i * chunks, (i + 1) * chunks)
        blocks = [
            attended_ref[here, :, g * INNER : (g + 1) * INNER].reshape(size, INNER) for g in range(GROUPS)
        ]
        for part in range(2):
            slot = len(copies)
            start = part * half * size
            attended = jnp.concatenate(blocks[part * half : (part + 1) * half], axis=0)
            result = dot_nn(attended, weight_ref[...])
            result = result + mixed_ref[start : start + half * size, :].astype(jnp.float32)
            block_ref[slot] = result.astype(jnp.bfloat16)
            there = pl.ds(pl.multiple_of(cam * rows + start, half * size), half * size)
            copies.append(pltpu.make_async_copy(block_ref.at[slot], out_hbm.at[there], sems.at[slot]))
            copies[-1].start()
    for copy in copies:
        copy.wait()


SMEM = pl.BlockSpec(memory_space=pltpu.SMEM)
VMEM = pl.BlockSpec(memory_space=pltpu.VMEM)
ANY = pl.BlockSpec(memory_space=pl.ANY)


def kernel_call(body, ins, outs, scratch, mib, flops, nbytes, out_space=VMEM):
    return pl.pallas_call(
        body,
        out_shape=outs,
        in_specs=ins,
        out_specs=[out_space] * len(outs),
        scratch_shapes=scratch,
        compiler_params=pltpu.CompilerParams(vmem_limit_bytes=mib * MIB),
        cost_estimate=pl.CostEstimate(flops=flops, bytes_accessed=nbytes, transcendentals=0),
    )


def shards(tokens, counts, neighbours, side_keys, cross_qkv, cross_out, time_qkv, time_out):
    cam_here, frames_here, token_count, model = tokens.shape
    cameras = cam_here * lax.axis_size("cam")
    frames = lax.axis_size("frame")
    rows = cam_here * token_count
    bf16 = jnp.bfloat16
    spread = functools.partial(jax.ShapeDtypeStruct, dtype=bf16)

    flat = tokens.reshape(rows, model)
    payload_lanes = GROUPS * model + LANES
    own_counts = counts.reshape(1, cam_here)
    cross_t, time_t = cross_qkv.T, time_qkv.T
    inside_pairs, early_pairs, late_pairs = exchange_pairs(lax.axis_size("cam"))
    sent = (token_count // 4 + 1, 4, model)

    outer, inner = kernel_call(
        norm_kernel, [SMEM, VMEM], [spread(sent)] * 2, [], 16, 6_000_000_000, 2_400_000
    )(own_counts, flat)
    early_far = lax.ppermute(outer, "cam", early_pairs)
    inner_far = lax.ppermute(inner, "cam", inside_pairs)

    query, part, info, mixed_inner, payload_inner = kernel_call(
        functools.partial(local_kernel, cameras),
        [SMEM, SMEM] + [VMEM] * 7,
        [
            jax.ShapeDtypeStruct((INNER, rows), jnp.float32),
            jax.ShapeDtypeStruct((HEADS, HEAD + 8, token_count), jnp.float32),
            jax.ShapeDtypeStruct((8, KEY_LANES), jnp.float32),
            spread((token_count, model)),
            spread((frames // 2, PLACES, payload_lanes)),
        ],
        [pltpu.VMEM((INNER, rows + token_count), jnp.float32)],
        36,
        8_000_000_000,
        20_000_000,
    )(own_counts, neighbours, outer, inner, inner_far, cross_t, side_keys, flat, cross_out)
    outer, payload_inner = lax.optimization_barrier((outer, payload_inner))
    late_far = lax.ppermute(outer, "cam", late_pairs)
    mixed_outer, payload = kernel_call(
        outer_kernel,
        [VMEM] * 9,
        [spread((token_count, model)), spread((frames, PLACES, payload_lanes))],
        [pltpu.VMEM((INNER, token_count), jnp.float32)],
        32,
        2_500_000_000,
        8_000_000,
    )(early_far, late_far, cross_t, info, query, part, flat, cross_out, payload_inner)

    arrived = to_owners(payload)
    (attended,) = kernel_call(
        functools.partial(time_kernel, frames),
        [VMEM] * 2,
        [spread((frames, PLACES, GROUPS * INNER))],
        [pltpu.VMEM((INNER, rows), jnp.float32)] * 2,
        32,
        6_000_000_000,
        10_000_000,
    )(arrived, time_t)
    returned = to_owners(attended)
    (out,) = kernel_call(
        final_kernel,
        [VMEM] * 4,
        [spread((rows, model))],
        [pltpu.VMEM((4, rows // 4, model), bf16), pltpu.SemaphoreType.DMA((4,))],
        32,
        700_000_000,
        4_000_000,
        ANY,
    )(returned, time_out, mixed_outer, mixed_inner)
    return out.reshape(tokens.shape)


def solution(mesh):
    return jax.shard_map(
        shards,
        mesh=mesh,
        in_specs=(
            P("cam", "frame", None, None),
            P("cam", "frame"),
            P("cam", None),
            P(),
            P(),
            P(),
            P(),
            P(),
        ),
        out_specs=P("cam", "frame", None, None),
        check_vma=False,
    )
```
